256 devices in a mesh: teacher: 8 (over z_hi, x), seq: 32 (over y, z_lo, core).
Axes of the slice: x: 4, y: 4, z: 8 (z_hi: 2, z_lo: 4; z = z_hi * 4 + z_lo), core: 2. Of those that a mesh axis runs over, the one named last changes fastest.
Arguments:
- tokens: bfloat16 [16384, 2048], P(('teacher', 'seq')), may hold values from -6 to 6
- router_weight: bfloat16 [2048, 64], replicated, may hold values from -0.25 to 0.25
- gate_weight: bfloat16 [64, 1536, 2048], P('seq', 'teacher'), may hold values from -0.125 to 0.125
- up_weight: bfloat16 [64, 1536, 2048], P('seq', 'teacher'), may hold values from -0.125 to 0.125
- down_weight: bfloat16 [64, 1536, 2048], P('seq', 'teacher'), may hold values from -0.15625 to 0.15625
- routing: int32 [16384, 2], P(('teacher', 'seq')), may hold values from 0 to 63, all different within a row; in each aligned block of 64 rows (0 to 63, 64 to 127, ...) at most 3 rows name the same one
- lengths: int32 [64], replicated, may hold values from 128 to 256, as said below
Outputs:
- mixed: bfloat16 [16384, 2048], P(('teacher', 'seq'))
The draws below stay inside these ranges and needn't reach their ends.
Inputs may be any that keep to these rules, and one draw needn't show every extreme that they name: `routing`: within the 64 rows of one device no expert is named more than 3 times, and in every draw some expert is named exactly 3 times there. `lengths`: some response window is fully live, 256 tokens.
All inputs are finite; a program needn't handle non-finite values.
Results may differ from the reference program's by a relative error of at most 0.017.
Values may be sent and summed in bfloat16 or wider, within the bound.
A program may use at most 64 MiB of HBM per device.

```python
import math
import jax
import jax.numpy as jnp
import numpy as np
from jax import lax

D = 2048
FF = 1536
TOP = 2
TOK_DEV = 64
EXPERTS = 64
CAP = 3
TOKENS = 16384
LENGTH = 256
RESP = 64
N_TEACHER = 8


def draw_lengths(key, part):
    key = jax.random.fold_in(key, 7)
    first_key, second_key = jax.random.split(key)
    drawn = jax.random.randint(first_key, (RESP,), LENGTH // 2, LENGTH + 1)
    longest = jax.random.randint(second_key, (), 0, RESP)
    return jnp.where(jnp.arange(RESP) == longest, LENGTH, drawn).astype(jnp.int32)


def block_scale(rng, dims, cuts, least, high):
    gain = 1.0
    for axis_at, blocks in cuts:
        steps = jax.random.uniform(jax.random.fold_in(jax.random.fold_in(rng, 6), axis_at), (blocks,), jnp.float32, least / len(cuts), high / len(cuts))
        gain = gain * jnp.repeat(jnp.exp(steps), dims[axis_at] // blocks).reshape((-1,) + (1,) * (len(dims) - 1 - axis_at))
    return gain


def shared_out(rng, own, number, rows, number_of, top, most, slope):
    order = jax.random.permutation(rng, number_of)
    crowded, common = portions_of(number_of, rows * top, most, slope, True), portions_of(number_of, rows * top, most, slope, False)
    places = jnp.arange(number_of)

    def named(tallies, offset_by):
        used = int((tallies > 0).sum())
        fixed = max(1, used // 4)
        moved = fixed + (places - fixed + offset_by * (used - fixed)) % max(1, number_of - fixed)
        return jnp.zeros((number_of,), jnp.int32).at[order[jnp.where(places < fixed, places, moved)]].set(jnp.asarray(tallies, jnp.int32))

    tallies = jnp.where(number % 4 == 0, named(crowded, number // 4), named(common, number - number // 4 - 1))
    mixed = jax.random.permutation(jax.random.fold_in(own, 3), number_of)
    donor, taker = mixed[0:number_of // 2 * 2:2], mixed[1:number_of // 2 * 2:2]
    slack = jnp.minimum(tallies[donor] - 1, most - tallies[taker]) // 2
    slack = jnp.where((donor == order[0]) | (taker == order[0]) | (tallies[taker] == 0), 0, jnp.maximum(slack, 0))
    moved = jax.random.randint(jax.random.fold_in(own, 4), (number_of // 2,), 0, 1 << 20) % (slack + 1)
    tallies = tallies.at[donor].add(-moved).at[taker].add(moved)
    members = jnp.searchsorted(jnp.cumsum(tallies), jnp.arange(rows * top), side="right").astype(jnp.int32)
    table = members.reshape(top, rows).T
    table = table[jax.random.permutation(jax.random.fold_in(own, 1), rows)]
    offset_by = jax.random.randint(jax.random.fold_in(own, 2), (rows, 1), 0, top)
    return jnp.take_along_axis(table, (jnp.arange(top)[None, :] + offset_by) % top, axis=1)


def portions_of(count, total, limit, skew, full):
    loads = [(1 << 20) // math.isqrt(standing ** skew) + 1 for standing in range(1, count + 1)]
    largest = limit if full else min(limit, max(-(-total // count), total * loads[0] // sum(loads)))
    least = 1 if total - largest >= count - 1 else 0
    counts, surplus = [largest] + [least] * (count - 1), total - largest - least * (count - 1)
    while surplus > 0:
        candidates = [i for i in range(1, count) if counts[i] < largest] or [i for i in range(1, count) if counts[i] < limit]
        whole, left = sum([loads[i] for i in candidates]), surplus
        for i in candidates:
            more = min(limit - counts[i], max(1, left * loads[i] // whole), surplus)
            counts[i] = counts[i] + more
            surplus = surplus - more
    return np.array(counts)


def normal_values(rng, extent, deviation, limit, shards=(), kind=jnp.bfloat16):
    values = jax.random.normal(rng, extent, jnp.float32) * deviation
    if len(shards) > 0:
        values = block_scale(rng, extent, shards, -0.22, 0.18) * values
    return jnp.clip(values, min=-limit, max=limit).astype(kind)


def setup_inputs(seed: int = 0) -> dict:
    splits = jax.random.split(jax.random.key(seed), 8)
    tokens = normal_values(splits[0], (TOKENS, D), 1.0, 6.0, ((0, 256),))
    router_weight = normal_values(splits[1], (D, EXPERTS), (D // 4) ** -0.5, 0.25)
    gate_weight = normal_values(splits[2], (EXPERTS, FF, D), D ** -0.5, 0.125, ((0, 32), (1, 8)))
    up_weight = normal_values(splits[3], (EXPERTS, FF, D), D ** -0.5, 0.125, ((0, 32), (1, 8)))
    down_weight = normal_values(splits[4], (EXPERTS, FF, D), FF ** -0.5, 0.15625, ((0, 32), (1, 8)))
    routing_keys = jax.random.split(jax.random.fold_in(splits[5], 1), TOKENS // TOK_DEV)
    routing_turns = jax.random.permutation(jax.random.fold_in(splits[5], 3), TOKENS // TOK_DEV)
    routing = jax.vmap(lambda own, number: shared_out(jax.random.fold_in(splits[5], 2), own, number, TOK_DEV, EXPERTS, TOP, CAP, 2))(routing_keys, routing_turns).reshape((TOKENS, TOP))
    lengths = draw_lengths(jax.random.fold_in(splits[7], 71), 0)
    return {"tokens": tokens, "router_weight": router_weight, "gate_weight": gate_weight, "up_weight": up_weight, "down_weight": down_weight, "routing": routing, "lengths": lengths}


def normalize(tokens):
    values = tokens.astype(jnp.float32)
    scale = lax.rsqrt(lax.optimization_barrier(jnp.mean(values * values, axis=-1, keepdims=True)) + 1e-06)
    return (values * scale).astype(jnp.bfloat16)

def expert_mlp(segment, gate_rows, up_rows, down_rows):
    gate = jnp.dot(segment, gate_rows.T, preferred_element_type=jnp.float32)
    upper = jnp.dot(segment, up_rows.T, preferred_element_type=jnp.float32)
    hidden = (jax.nn.silu(gate) * upper).astype(jnp.bfloat16)
    width = gate_rows.shape[0] // N_TEACHER
    hidden_split = hidden.reshape(segment.shape[0], N_TEACHER, width).astype(jnp.float32)
    down_split = down_rows.reshape(N_TEACHER, width, down_rows.shape[1]).astype(jnp.float32)
    parts = jnp.einsum('rjf,jfd->jrd', hidden_split, down_split).astype(jnp.bfloat16)
    parts = lax.optimization_barrier(parts).astype(jnp.float32)
    return lax.optimization_barrier(jnp.sum(parts, axis=0)).astype(jnp.bfloat16)

def reference(tokens, router_weight, gate_weight, up_weight, down_weight, routing, lengths):
    normed = normalize(tokens)
    logits = jnp.dot(normed, router_weight, preferred_element_type=jnp.float32)
    chosen = jnp.take_along_axis(logits, routing, axis=1)
    scores = jax.nn.sigmoid(chosen)
    position = jnp.arange(TOKENS, dtype=jnp.int32)
    response = position // LENGTH
    offset = position - response * LENGTH
    is_live = offset < lengths[response]
    route_weight = jnp.where(is_live[:, None], scores / lax.optimization_barrier(jnp.sum(scores, axis=1, keepdims=True)), jnp.zeros((), jnp.float32))
    blocks = TOKENS // TOK_DEV
    slots_all = EXPERTS * CAP
    flat_ids = routing.reshape(blocks, TOK_DEV * TOP)
    flat_live = jnp.repeat(is_live, TOP).reshape(blocks, TOK_DEV * TOP)
    onehot = ((flat_ids[:, :, None] == jnp.arange(EXPERTS, dtype=jnp.int32)[None, None, :]) & flat_live[:, :, None]).astype(jnp.int32)
    ranking = jnp.cumsum(onehot, axis=1) - onehot
    slot_ids = lax.optimization_barrier(jnp.sum(ranking * onehot, axis=2)).astype(jnp.int32)
    target = jnp.where(flat_live, flat_ids * CAP + slot_ids, slots_all).astype(jnp.int32)
    token_of = jnp.broadcast_to(jnp.repeat(jnp.arange(TOK_DEV, dtype=jnp.int32), TOP)[None, :], target.shape)
    block_of = jnp.broadcast_to(jnp.arange(blocks, dtype=jnp.int32)[:, None], target.shape)
    slot_table = jnp.full((blocks, slots_all + 1), -1, jnp.int32).at[block_of, target].set(token_of)[:, :slots_all]
    block_rows = normed.reshape(blocks, TOK_DEV, D)
    block_index = jnp.arange(blocks, dtype=jnp.int32)[:, None]
    gathered = block_rows[block_index, jnp.maximum(slot_table, 0)]
    gathered = jnp.where((slot_table >= 0)[:, :, None], gathered, jnp.zeros((), jnp.bfloat16))
    by_expert = gathered.reshape(blocks, EXPERTS, CAP, D).transpose(1, 0, 2, 3).reshape(EXPERTS, blocks * CAP, D)
    expert_out = lax.map(lambda packed: expert_mlp(packed[0], packed[1], packed[2], packed[3]), (by_expert, gate_weight, up_weight, down_weight))
    restored = expert_out.reshape(EXPERTS, blocks, CAP, D).transpose(1, 0, 2, 3).reshape(blocks, slots_all, D)
    picked = restored[block_index, jnp.minimum(target, slots_all - 1)].reshape(TOKENS, TOP, D)
    mixed = lax.optimization_barrier(jnp.sum(picked.astype(jnp.float32) * route_weight[:, :, None], axis=1))
    return mixed.astype(jnp.bfloat16)
```

```python
import functools

import jax
import jax.numpy as jnp
from jax import lax
from jax.experimental import pallas as pl
from jax.experimental.pallas import tpu as pltpu
from jax.sharding import PartitionSpec as P

MESH = pl.DeviceIdType.MESH
NX, NY, NZ, NLO = 4, 4, 8, 4
CHIPS = NX * NY * NZ
LANE = 128
SUB = 16


def normalize(tokens):
    values = tokens.astype(jnp.float32)
    scale = lax.rsqrt(jnp.mean(values * values, axis=-1, keepdims=True) + 1e-06)
    return (values * scale).astype(jnp.bfloat16)


def plan_routes(
    normed, router_weight, routing, lengths, block_index, length_all, experts, capacity
):
    tok_dev = normed.shape[0]
    top_count = routing.shape[1]
    logits = jnp.dot(normed, router_weight, preferred_element_type=jnp.float32)
    expert_ids = jnp.arange(experts, dtype=jnp.int32)
    named = routing[:, :, None] == expert_ids[None, None, :]
    chosen = jnp.sum(jnp.where(named, logits[:, None, :], 0.0), axis=2)
    scores = jax.nn.sigmoid(chosen)
    position = block_index * tok_dev + jnp.arange(tok_dev, dtype=jnp.int32)
    response = position // length_all
    offset = position - response * length_all
    limit = jnp.sum(
        jnp.where(
            response[:, None] == jnp.arange(lengths.shape[0], dtype=jnp.int32)[None, :],
            lengths[None, :],
            0,
        ),
        axis=1,
    )
    is_live = offset < limit
    route_weight = jnp.where(
        is_live[:, None],
        scores / jnp.sum(scores, axis=1, keepdims=True),
        jnp.zeros((), jnp.float32),
    )
    hits = jnp.any(named, axis=1) & is_live[:, None]
    earlier = jnp.arange(tok_dev)[:, None] > jnp.arange(tok_dev)[None, :]
    rank = jnp.dot(
        earlier.astype(jnp.bfloat16), hits.astype(jnp.bfloat16),
        preferred_element_type=jnp.float32,
    ).astype(jnp.int32)
    slot_ids = jnp.sum(jnp.where(named, rank[:, None, :], 0), axis=2)
    target = jnp.where(is_live[:, None], routing * capacity + slot_ids, -1)
    flat = target.reshape(-1)
    owner = jnp.arange(tok_dev * top_count, dtype=jnp.int32) // top_count
    slots = jnp.arange(experts * capacity, dtype=jnp.int32)
    table = jnp.sum(jnp.where(flat[None, :] == slots[:, None], owner[None, :], 0), axis=1)
    return table, jnp.maximum(flat, 0), route_weight.reshape(-1)


def place(sid):
    return sid % NX, sid // (NX * NZ), (sid // NX) % NZ


def device(x, y, z, core):
    return ((z // NLO) * NX + x, (y * NLO + z % NLO) * 2 + core)


def kernel(
    table_ref, target_ref, weight_ref, tok_ref, gate_ref, up_ref, down_ref, out_ref,
    send, recv, rows_in, wbuf, hidden, stage, rsend, back,
    w_send, w_recv, f_send, f_recv, t_send, t_recv, r_send, r_recv,
):
    teacher, seq = lax.axis_index("teacher"), lax.axis_index("seq")
    x, z_hi = teacher % NX, teacher // NX
    core, z_lo, y = seq % 2, (seq // 2) % NLO, seq // (2 * NLO)
    z = z_hi * NLO + z_lo
    me = (y * NZ + z) * NX + x
    my_expert = (y * NLO + z_lo) * NX + x
    depth = gate_ref.shape[1]
    half = depth // 2
    cap = send.shape[1]
    chunk_src = CHIPS // NY
    chunk_rows = chunk_src * cap

    barrier = pltpu.get_barrier_semaphore()

    @pl.loop(1, CHIPS)
    def _(i):
        px, py, pz = place((me + i) % CHIPS)
        pl.semaphore_signal(
            barrier, inc=1, device_id=device(px, py, pz, core), device_id_type=MESH
        )

    for px in range(NX):
        pl.semaphore_signal(
            barrier, inc=1, device_id=device(px, y, z, 1 - core), device_id_type=MESH
        )
    pl.semaphore_wait(barrier, CHIPS - 1 + NX)

    weights = (gate_ref, up_ref, down_ref)
    for i in range(2):
        goal = 2 * core + i

        @pl.when(goal != x)
        def _():
            for part in range(2):
                for m in range(3):
                    pltpu.make_async_remote_copy(
                        src_ref=weights[m].at[i, pl.ds(part * half, half), :],
                        dst_ref=wbuf.at[x, m, pl.ds(part * half, half), :],
                        send_sem=w_send,
                        recv_sem=w_recv.at[x],
                        device_id=device(goal, y, z, part),
                        device_id_type=MESH,
                    ).start()

        @pl.when(goal == x)
        def _():
            for m in range(3):
                pltpu.make_async_copy(weights[m].at[i], wbuf.at[x, m], w_recv.at[x]).start()
                pltpu.make_async_remote_copy(
                    src_ref=weights[m].at[i],
                    dst_ref=wbuf.at[x, m],
                    send_sem=w_send,
                    recv_sem=w_recv.at[x],
                    device_id=device(x, y, z, 1 - core),
                    device_id_type=MESH,
                ).start()

    experts = send.shape[0]

    @pl.loop(0, experts)
    def _(e):
        for r in range(cap):
            send[e, r] = tok_ref[table_ref[e * cap + r]]

    pltpu.make_async_copy(send.at[my_expert], recv.at[me], t_recv).start()

    @pl.loop(1, CHIPS)
    def _(i):
        px, py, pz = place((me + i) % CHIPS)
        pltpu.make_async_remote_copy(
            src_ref=send.at[(py * NLO + pz % NLO) * NX + px],
            dst_ref=recv.at[me],
            send_sem=t_send,
            recv_sem=t_recv,
            device_id=device(px, py, pz, core),
            device_id_type=MESH,
        ).start()

    def half_of(s, part):
        return wbuf.at[s, :, pl.ds(part * half, half), :]

    def forward(d):
        s = (x + d) % NX
        mine = half_of(s, core)
        pltpu.make_async_copy(mine, mine, w_recv.at[s]).wait()
        pltpu.make_async_remote_copy(
            src_ref=mine,
            dst_ref=mine,
            send_sem=f_send.at[s],
            recv_sem=f_recv.at[s],
            device_id=device(x, y, z, 1 - core),
            device_id_type=MESH,
        ).start()

    def first_layer(d):
        s = (x + d) % NX
        if d == 0:
            pltpu.make_async_copy(wbuf.at[s], wbuf.at[s], w_recv.at[s]).wait()
        else:
            other = half_of(s, 1 - core)
            pltpu.make_async_copy(other, other, f_recv.at[s]).wait()

        @pl.loop(0, rows_in.shape[0] // 128)
        def _(b):
            at = pl.ds(pl.multiple_of(b * 128, 128), 128)
            block = rows_in[at, :]
            dims = (((1,), (1,)), ((), ()))
            gate = lax.dot_general(block, wbuf[s, 0], dims, preferred_element_type=jnp.float32)
            upper = lax.dot_general(block, wbuf[s, 1], dims, preferred_element_type=jnp.float32)
            hidden[s, at, :] = (gate / (1.0 + jnp.exp(-gate)) * upper).astype(jnp.bfloat16)

    forward(1)
    forward(3)

    pltpu.make_async_copy(recv, recv, t_recv).wait()

    @pl.loop(0, NY)
    def _(g):
        part = recv[pl.ds(g * chunk_src, chunk_src)]
        stage[...] = part.reshape(chunk_rows * SUB, LANE).astype(jnp.float32)
        at = pl.ds(pl.multiple_of(g * chunk_rows, chunk_rows), chunk_rows)
        for k in range(SUB):
            rows_in[at, k * LANE:(k + 1) * LANE] = stage[
                pl.ds(k, chunk_rows, stride=SUB), :
            ].astype(jnp.bfloat16)

    first_layer(0)
    first_layer(1)
    first_layer(3)
    forward(2)
    first_layer(2)

    @pl.loop(0, NY)
    def _(i):
        g = (y + i) % NY
        at = pl.ds(pl.multiple_of(g * chunk_rows, chunk_rows), chunk_rows)
        wide = 512
        for n in range(SUB * LANE // wide):
            total = jnp.zeros((chunk_rows, wide), jnp.float32)
            for s in range(NX):
                total += jnp.dot(
                    hidden[s, at, :], wbuf[s, 2, :, n * wide:(n + 1) * wide],
                    preferred_element_type=jnp.float32,
                )
            for k in range(wide // LANE):
                stage[pl.ds(n * (wide // LANE) + k, chunk_rows, stride=SUB), :] = total[
                    :, k * LANE:(k + 1) * LANE
                ]
        rsend[pl.ds(g * chunk_src, chunk_src)] = (
            stage[...].astype(jnp.bfloat16).reshape(chunk_src, cap, SUB, LANE)
        )

        @pl.loop(0, chunk_src)
        def _(j):
            sid = g * chunk_src + (me + j) % chunk_src
            px, py, pz = place(sid)

            @pl.when(sid != me)
            def _():
                pltpu.make_async_remote_copy(
                    src_ref=rsend.at[sid],
                    dst_ref=back.at[z_hi, my_expert],
                    send_sem=r_send,
                    recv_sem=r_recv,
                    device_id=device(px, py, pz, core),
                    device_id_type=MESH,
                ).start()

            @pl.when(sid == me)
            def _():
                pltpu.make_async_copy(rsend.at[sid], back.at[z_hi, my_expert], r_recv).start()

    pltpu.make_async_copy(back, back, r_recv).wait()

    tokens = tok_ref.shape[0]

    @pl.loop(0, tokens)
    def _(t):
        total = jnp.zeros((SUB, LANE), jnp.float32)
        for k in range(2):
            slot = target_ref[2 * t + k]
            e, r = slot // cap, slot % cap
            total += weight_ref[2 * t + k] * (
                back[0, e, r].astype(jnp.float32) + back[1, e, r].astype(jnp.float32)
            )
        out_ref[t] = total.astype(jnp.bfloat16)

    others = pl.ds(0, CHIPS - 1)
    pltpu.make_async_copy(recv.at[others], recv.at[others], t_send).wait()
    pltpu.make_async_copy(rsend.at[others], rsend.at[others], r_send).wait()
    two = pl.ds(0, 2)
    pltpu.make_async_copy(wbuf.at[two], wbuf.at[two], w_send).wait()
    for d in range(1, NX):
        s = (x + d) % NX
        mine = half_of(s, core)
        pltpu.make_async_copy(mine, mine, f_send.at[s]).wait()


def local(tokens, router_weight, gate_weight, up_weight, down_weight, routing, lengths):
    tok_dev, width = tokens.shape
    top_count = routing.shape[1]
    seq_size = lax.axis_size("seq")
    experts = gate_weight.shape[0] * seq_size
    depth = gate_weight.shape[1]
    capacity = max(2, tok_dev * top_count // experts + 1)
    length_all = 4 * tok_dev
    block_index = lax.axis_index("teacher") * seq_size + lax.axis_index("seq")
    normed = normalize(tokens)
    table, target, route_weight = plan_routes(
        normed, router_weight, routing, lengths, block_index, length_all, experts, capacity
    )
    rows = CHIPS * capacity
    smem = pl.BlockSpec(memory_space=pltpu.SMEM)
    vmem = pl.BlockSpec(memory_space=pltpu.VMEM)
    hbm = pl.BlockSpec(memory_space=pl.ANY)
    sem = pltpu.SemaphoreType.DMA
    bf16 = jnp.bfloat16
    mixed = pl.pallas_call(
        kernel,
        out_shape=jax.ShapeDtypeStruct((tok_dev, SUB, LANE), bf16),
        in_specs=[smem, smem, smem, vmem, hbm, hbm, hbm],
        out_specs=vmem,
        scratch_shapes=[
            pltpu.VMEM((experts, capacity, SUB, LANE), bf16),
            pltpu.VMEM((CHIPS, capacity, SUB, LANE), bf16),
            pltpu.VMEM((rows, width), bf16),
            pltpu.VMEM((NX, 3, depth, width), bf16),
            pltpu.VMEM((NX, rows, depth), bf16),
            pltpu.VMEM((rows // NY * SUB, LANE), jnp.float32),
            pltpu.VMEM((CHIPS, capacity, SUB, LANE), bf16),
            pltpu.VMEM((2, experts, capacity, SUB, LANE), bf16),
            sem, sem((NX,)), sem((NX,)), sem((NX,)), sem, sem, sem, sem,
        ],
        compiler_params=pltpu.CompilerParams(
            collective_id=0, has_side_effects=True, vmem_limit_bytes=48 * 1024 * 1024
        ),
    )(
        table, target, route_weight, normed.reshape(tok_dev, SUB, LANE),
        gate_weight, up_weight, down_weight,
    )
    return mixed.reshape(tok_dev, width)


def solution(mesh):
    in_specs = (
        P(("teacher", "seq"), None),
        P(),
        P("seq", "teacher", None),
        P("seq", "teacher", None),
        P("seq", "teacher", None),
        P(("teacher", "seq"), None),
        P(),
    )
    out_specs = P(("teacher", "seq"), None)
    return jax.shard_map(local, mesh=mesh, in_specs=in_specs, out_specs=out_specs, check_vma=False)
```

```python
import jax
import jax.numpy as jnp
from jax import lax
from jax.experimental import pallas as pl
from jax.experimental.pallas import tpu as pltpu
from jax.sharding import PartitionSpec as P

MESH = pl.DeviceIdType.MESH
NX, NY, NZ, NLO = 4, 4, 8, 4
PLANE = NX * NY
LANE = 128
SUB = 16
CHUNKS = 4
ORDER = (1, 3, 2)


def device(x, y, z, core):
    return ((z // NLO) * NX + x, (y * NLO + z % NLO) * 2 + core)


def split(values, by):
    if by == 16:
        whole = lax.shift_right_logical(values, 4)
    else:
        whole = lax.shift_right_logical(values * 171, {3: 9, 12: 11, 48: 13}[by])
    return whole, values - whole * by


def slot_columns(shape, per_place, cap):
    place, left = split(lax.broadcasted_iota(jnp.int32, shape, 1), per_place)
    z_lo, rank = split(left, cap)
    y, x = lax.shift_right_logical(place, 2), place & (NX - 1)
    expert = jnp.where(left < NLO * cap, (y * NLO + z_lo) * NX + x, -1)
    return expert, rank


def copy(src, dst, sem):
    return pltpu.make_async_copy(src, dst, sem)


def push(src, dst, send_sem, recv_sem, to):
    pltpu.make_async_remote_copy(
        src_ref=src, dst_ref=dst, send_sem=send_sem, recv_sem=recv_sem,
        device_id=to, device_id_type=MESH,
    ).start()


def take(ref, sem):
    pltpu.make_async_copy(ref, ref, sem).wait()


def kernel(
    lengths_ref, tok_ref, router_ref, routing_ref, gate_ref, up_ref, down_ref, out_ref,
    normed, mix_hi, mix_lo, order, gather, send1, plane_in, recv, rows_in, gate_up, down,
    hidden, sorted_hidden, stage, rsend, z_back, xsend, back,
    g_send, g_recv, gf_send, gf_recv, d_send, d_recv, df_send, df_recv,
    p_send, p_recv, z_send, z_recv, rz_send, rz_recv, rp_send, rp_recv,
):
    f32, bf16 = jnp.float32, jnp.bfloat16
    teacher, seq = lax.axis_index("teacher"), lax.axis_index("seq")
    x, z_hi = teacher % NX, teacher // NX
    core, z_lo, y = seq % 2, (seq // 2) % NLO, seq // (2 * NLO)
    z = z_hi * NLO + z_lo
    here = y * NX + x
    sibling = device(x, y, z, 1 - core)
    tokens, width = tok_ref.shape
    depth = gate_ref.shape[1]
    half = depth // 2
    cap = send1.shape[2]
    wide = width // CHUNKS
    rows = rows_in.shape[0]
    group = rows // NY
    per_z = rows // NZ

    barrier = pltpu.get_barrier_semaphore()

    def greet(to):
        pl.semaphore_signal(barrier, inc=1, device_id=to, device_id_type=MESH)

    @pl.loop(0, NX)
    def _(px):
        greet(device(px, y, z, 1 - core))

    @pl.loop(1, PLANE)
    def _(i):
        at = (here + i) % PLANE
        greet(device(at % NX, at // NX, z, core))

    @pl.loop(1, NZ)
    def _(i):
        greet(device(x, y, (z + i) % NZ, core))

    pl.semaphore_wait(barrier, NX + PLANE - 1 + NZ - 1)

    def send_gate_up(i, m, part):
        ref = (gate_ref, up_ref)[m]
        goal = 2 * core + i
        at = pl.ds(part * half, half)

        @pl.when(goal != x)
        def _():
            push(
                ref.at[i, at, :], gate_up.at[x, m, at, :], g_send, g_recv.at[x],
                device(goal, y, z, part),
            )

        @pl.when(goal == x)
        def _():
            copy(ref.at[i, at, :], gate_up.at[x, m, at, :], g_recv.at[x]).start()
            push(ref.at[i, at, :], gate_up.at[x, m, at, :], g_send, g_recv.at[x], sibling)

    def send_down(i, c, part):
        goal = 2 * core + i
        at, cols = pl.ds(part * half, half), pl.ds(c * wide, wide)

        @pl.when(goal != x)
        def _():
            push(
                down_ref.at[i, at, cols], down.at[x, at, cols], d_send, d_recv.at[x, c],
                device(goal, y, z, part),
            )

        @pl.when(goal == x)
        def _():
            copy(down_ref.at[i, at, cols], down.at[x, at, cols], d_recv.at[x, c]).start()
            push(down_ref.at[i, at, cols], down.at[x, at, cols], d_send, d_recv.at[x, c], sibling)

    for i in range(2):
        send_gate_up(i, 0, 0)

    values = tok_ref[...].astype(f32)
    scale = lax.rsqrt(jnp.mean(values * values, axis=-1, keepdims=True) + 1e-06)
    normed[...] = (values * scale).astype(bf16)
    block = teacher * (2 * NLO * NY) + seq
    first = (block % 4) * tokens
    limit = lengths_ref[block // 4]
    live = first + lax.broadcasted_iota(jnp.int32, (tokens, 1), 0) < limit
    name0, name1 = routing_ref[:, 0:1], routing_ref[:, 1:2]
    earlier = (
        lax.broadcasted_iota(jnp.int32, (tokens, tokens), 0)
        > lax.broadcasted_iota(jnp.int32, (tokens, tokens), 1)
    ).astype(f32).astype(bf16)

    def slots(count, per_place):
        expert, rank = slot_columns((tokens, count), per_place, cap)
        named = jnp.logical_or(name0 == expert, name1 == expert)
        hit = jnp.where(jnp.logical_and(named, live), 1.0, 0.0)
        before = jnp.dot(earlier, hit.astype(bf16), preferred_element_type=f32)
        return expert, jnp.where(before == rank.astype(f32), hit, 0.0)

    _, chosen = slots(PLANE * NLO * cap, NLO * cap)
    picked = lax.dot_general(
        chosen.astype(bf16), normed[...], (((0,), (0,)), ((), ())), preferred_element_type=f32
    )
    for k in range(SUB):
        stage[pl.ds(k, PLANE * NLO * cap, stride=SUB), :] = picked[:, k * LANE:(k + 1) * LANE]
    send1[...] = stage[...].astype(bf16).reshape(send1.shape)

    copy(send1.at[here], plane_in.at[here], p_recv.at[y]).start()

    @pl.loop(1, PLANE)
    def _(i):
        at = (here + i) % PLANE
        push(
            send1.at[at], plane_in.at[here], p_send, p_recv.at[y],
            device(at % NX, at // NX, z, core),
        )

    for i in range(2):
        send_gate_up(i, 0, 1)
    for part in range(2):
        for i in range(2):
            send_gate_up(i, 1, part)
    for c in range(CHUNKS):
        for part in range(2):
            for i in range(2):
                send_down(i, c, part)

    logits = jnp.dot(normed[...], router_ref[...], preferred_element_type=f32)
    ids = lax.broadcasted_iota(jnp.int32, logits.shape, 1)

    def score(name):
        return jax.nn.sigmoid(
            jnp.sum(jnp.where(name == ids, logits, 0.0), axis=1, keepdims=True)
        )

    score0, score1 = score(name0), score(name1)
    both = score0 + score1
    expert, used = slots(PLANE * SUB, SUB)
    mix = used * jnp.where(name0 == expert, score0 / both, score1 / both)
    high = mix.astype(bf16)
    mix_hi[...] = high
    mix_lo[...] = (mix - high.astype(f32)).astype(bf16)

    @pl.loop(0, NY)
    def _(i):
        g = (y + i) % NY
        at = pl.ds(g * NX, NX)
        take(plane_in.at[at], p_recv.at[g])
        copy(plane_in.at[at, z_lo], recv.at[g, z], z_recv.at[g]).start()

        @pl.loop(1, NZ)
        def _(j):
            pz = (z + j) % NZ
            push(
                plane_in.at[at, pz % NLO], recv.at[g, z], z_send, z_recv.at[g],
                device(x, y, pz, core),
            )

    i_at, q = split(lax.broadcasted_iota(jnp.int32, (rows, rows), 0), per_z)
    by_y, rest = split(q, NX * cap)
    column = lax.broadcasted_iota(jnp.int32, (rows, rows), 1)
    order[...] = (by_y * group + i_at * (NX * cap) + rest == column).astype(f32).astype(bf16)
    place, left = split(lax.broadcasted_iota(jnp.int32, (PLANE * SUB, rows), 0), SUB)
    from_z, q = split(lax.broadcasted_iota(jnp.int32, (PLANE * SUB, rows), 1), per_z)
    to_place, rank = split(q, cap)
    same = jnp.logical_and(place == to_place, left == (from_z & (NLO - 1)) * cap + rank)
    gather[...] = same.astype(f32).astype(bf16)

    def relayout(i):
        g = (y + i) % NY
        take(recv.at[g], z_recv.at[g])
        part = pl.ds(0, group * SUB)
        stage[part, :] = recv[g].reshape(group * SUB, LANE).astype(f32)
        at = pl.ds(pl.multiple_of(g * group, group), group)
        for k in range(SUB):
            rows_in[at, k * LANE:(k + 1) * LANE] = stage[
                pl.ds(k, group, stride=SUB), :
            ].astype(bf16)

    def first_layer(i):
        g = (y + i) % NY
        at = pl.ds(pl.multiple_of(g * group, group), group)
        block = rows_in[at, :]

        @pl.loop(0, NX)
        def _(s):
            dims = (((1,), (1,)), ((), ()))
            gate = lax.dot_general(block, gate_up[s, 0], dims, preferred_element_type=f32)
            upper = lax.dot_general(block, gate_up[s, 1], dims, preferred_element_type=f32)
            hidden[s, at, :] = (gate / (1.0 + jnp.exp(-gate)) * upper).astype(bf16)

    def gate_half(s, part):
        return gate_up.at[s, :, pl.ds(part * half, half), :]

    def down_half(s, c, part):
        return down.at[s, pl.ds(part * half, half), pl.ds(c * wide, wide)]

    for i in range(2):
        relayout(i)

    for d in ORDER:
        s = (x + d) % NX
        mine = gate_half(s, core)
        take(mine, g_recv.at[s])
        push(mine, mine, gf_send.at[s], gf_recv.at[s], sibling)
    take(gate_up.at[x], g_recv.at[x])
    for d in ORDER:
        s = (x + d) % NX
        take(gate_half(s, 1 - core), gf_recv.at[s])

    for i in range(2):
        first_layer(i)
    for i in range(2, 4):
        relayout(i)
    for i in range(2, 4):
        first_layer(i)

    @pl.loop(0, NX)
    def _(s):
        sorted_hidden[s] = jnp.dot(
            order[...], hidden[s], preferred_element_type=f32
        ).astype(bf16)

    for c in range(CHUNKS):
        for d in ORDER:
            s = (x + d) % NX
            mine = down_half(s, c, core)
            take(mine, d_recv.at[s, c])
            push(mine, mine, df_send.at[s, c], df_recv.at[s, c], sibling)
        cols = pl.ds(c * wide, wide)
        take(down.at[x, :, cols], d_recv.at[x, c])
        for d in ORDER:
            s = (x + d) % NX
            take(down_half(s, c, 1 - core), df_recv.at[s, c])

        @pl.loop(0, rows // 128)
        def _(b):
            at = pl.ds(pl.multiple_of(b * 128, 128), 128)
            total = jnp.zeros((128, wide), f32)
            for s in range(NX):
                total += jnp.dot(
                    sorted_hidden[s, at, :], down[s, :, c * wide:(c + 1) * wide],
                    preferred_element_type=f32,
                )
            rsend[c, at, :] = total.astype(bf16)

        def mine_of(pz):
            return rsend.at[c, pl.ds(pl.multiple_of(pz * per_z, per_z), per_z), :]

        copy(mine_of(z), z_back.at[c, pl.ds(pl.multiple_of(z * per_z, per_z), per_z), :],
             rz_recv.at[c]).start()

        @pl.loop(1, NZ)
        def _(j):
            pz = (z + j) % NZ
            push(
                mine_of(pz),
                z_back.at[c, pl.ds(pl.multiple_of(z * per_z, per_z), per_z), :],
                rz_send, rz_recv.at[c], device(x, y, pz, core),
            )

    def finish(c):
        take(back.at[c], rp_recv.at[c])
        total = jnp.dot(mix_hi[...], back[c], preferred_element_type=f32)
        total += jnp.dot(mix_lo[...], back[c], preferred_element_type=f32)
        out_ref[:, c * wide:(c + 1) * wide] = total.astype(bf16)

    for c in range(CHUNKS):
        take(z_back.at[c], rz_recv.at[c])
        xsend[c] = jnp.dot(gather[...], z_back[c], preferred_element_type=f32).astype(bf16)
        landing = back.at[c, pl.ds(pl.multiple_of(here * SUB, SUB), SUB), :]
        copy(
            xsend.at[c, pl.ds(pl.multiple_of(here * SUB, SUB), SUB), :], landing, rp_recv.at[c]
        ).start()

        @pl.loop(1, PLANE)
        def _(i):
            at = (here + i) % PLANE
            push(
                xsend.at[c, pl.ds(pl.multiple_of(at * SUB, SUB), SUB), :], landing,
                rp_send, rp_recv.at[c], device(at % NX, at // NX, z, core),
            )

        if c > 0:
            finish(c - 1)
    finish(CHUNKS - 1)

    take(plane_in.at[pl.ds(0, PLANE - 1)], p_send)
    take(recv.at[:, pl.ds(0, NZ - 1)], z_send)
    take(z_back.at[:, pl.ds(0, rows - per_z), :], rz_send)
    take(back.at[:, pl.ds(0, (PLANE - 1) * SUB), :], rp_send)
    take(gate_up.at[pl.ds(0, 2)], g_send)
    take(down.at[pl.ds(0, 2)], d_send)
    for d in ORDER:
        s = (x + d) % NX
        take(gate_half(s, core), gf_send.at[s])
        for c in range(CHUNKS):
            take(down_half(s, c, core), df_send.at[s, c])


def local(tokens, router_weight, gate_weight, up_weight, down_weight, routing, lengths):
    tok_dev, width = tokens.shape
    top_count = routing.shape[1]
    experts = gate_weight.shape[0] * lax.axis_size("seq")
    depth = gate_weight.shape[1]
    cap = max(2, tok_dev * top_count // experts + 1)
    rows = PLANE * NZ * cap
    wide = width // CHUNKS
    smem = pl.BlockSpec(memory_space=pltpu.SMEM)
    vmem = pl.BlockSpec(memory_space=pltpu.VMEM)
    hbm = pl.BlockSpec(memory_space=pl.ANY)
    sem = pltpu.SemaphoreType.DMA
    bf16 = jnp.bfloat16
    return pl.pallas_call(
        kernel,
        out_shape=jax.ShapeDtypeStruct((tok_dev, width), bf16),
        in_specs=[smem, vmem, vmem, vmem, hbm, hbm, hbm],
        out_specs=vmem,
        scratch_shapes=[
            pltpu.VMEM((tok_dev, width), bf16),
            pltpu.VMEM((tok_dev, PLANE * SUB), bf16),
            pltpu.VMEM((tok_dev, PLANE * SUB), bf16),
            pltpu.VMEM((rows, rows), bf16),
            pltpu.VMEM((PLANE * SUB, rows), bf16),
            pltpu.VMEM((PLANE, NLO, cap, SUB, LANE), bf16),
            pltpu.VMEM((PLANE, NLO, cap, SUB, LANE), bf16),
            pltpu.VMEM((NY, NZ, NX, cap, SUB, LANE), bf16),
            pltpu.VMEM((rows, width), bf16),
            pltpu.VMEM((NX, 2, depth, width), bf16),
            pltpu.VMEM((NX, depth, width), bf16),
            pltpu.VMEM((NX, rows, depth), bf16),
            pltpu.VMEM((NX, rows, depth), bf16),
            pltpu.VMEM((PLANE * NLO * cap * SUB, LANE), jnp.float32),
            pltpu.VMEM((CHUNKS, rows, wide), bf16),
            pltpu.VMEM((CHUNKS, rows, wide), bf16),
            pltpu.VMEM((CHUNKS, PLANE * SUB, wide), bf16),
            pltpu.VMEM((CHUNKS, PLANE * SUB, wide), bf16),
            sem, sem((NX,)), sem((NX,)), sem((NX,)),
            sem, sem((NX, CHUNKS)), sem((NX, CHUNKS)), sem((NX, CHUNKS)),
            sem, sem((NY,)), sem, sem((NY,)),
            sem, sem((CHUNKS,)), sem, sem((CHUNKS,)),
        ],
        compiler_params=pltpu.CompilerParams(
            collective_id=0, has_side_effects=True, vmem_limit_bytes=48 * 1024 * 1024
        ),
    )(lengths, tokens, router_weight, routing, gate_weight, up_weight, down_weight)


def solution(mesh):
    in_specs = (
        P(("teacher", "seq"), None),
        P(),
        P("seq", "teacher", None),
        P("seq", "teacher", None),
        P("seq", "teacher", None),
        P(("teacher", "seq"), None),
        P(),
    )
    out_specs = P(("teacher", "seq"), None)
    return jax.shard_map(local, mesh=mesh, in_specs=in_specs, out_specs=out_specs, check_vma=False)
```

```python
import jax
import jax.numpy as jnp
from jax import lax
from jax.experimental import pallas as pl
from jax.experimental.pallas import tpu as pltpu
from jax.sharding import PartitionSpec as P

MESH = pl.DeviceIdType.MESH
NX, NY, NZ, NLO = 4, 4, 8, 4
PLANE = NX * NY
LANE = 128
SUB = 16
CHUNKS = 4
ORDER = (1, 3, 2)


def device(x, y, z, core):
    return ((z // NLO) * NX + x, (y * NLO + z % NLO) * 2 + core)


def split(values, by):
    if by == 16:
        whole = lax.shift_right_logical(values, 4)
    else:
        whole = lax.shift_right_logical(values * 171, {3: 9, 12: 11, 48: 13}[by])
    return whole, values - whole * by


def slot_columns(shape, per_place, cap):
    place, left = split(lax.broadcasted_iota(jnp.int32, shape, 1), per_place)
    z_lo, rank = split(left, cap)
    y, x = lax.shift_right_logical(place, 2), place & (NX - 1)
    expert = jnp.where(left < NLO * cap, (y * NLO + z_lo) * NX + x, -1)
    return expert, rank


def copy(src, dst, sem):
    return pltpu.make_async_copy(src, dst, sem)


def push(src, dst, send_sem, recv_sem, to):
    pltpu.make_async_remote_copy(
        src_ref=src, dst_ref=dst, send_sem=send_sem, recv_sem=recv_sem,
        device_id=to, device_id_type=MESH,
    ).start()


def take(ref, sem):
    pltpu.make_async_copy(ref, ref, sem).wait()


def kernel(
    lengths_hbm, tok_hbm, router_hbm, routing_hbm, gate_ref, up_ref, down_ref, out_ref,
    lengths_ref, tok_ref, router_ref, routing_ref, normed, mix_hi, mix_lo, order, gather, send1, plane_in, recv, rows_in, gate_up, down,
    hidden, sorted_hidden, stage, rsend, z_back, xsend, back,
    g_send, g_recv, gf_send, gf_recv, d_send, d_recv, df_send, df_recv,
    p_send, p_recv, z_send, z_recv, rz_send, rz_recv, rp_send, rp_recv, in_sem,
):
    f32, bf16 = jnp.float32, jnp.bfloat16
    teacher, seq = lax.axis_index("teacher"), lax.axis_index("seq")
    x, z_hi = teacher % NX, teacher // NX
    core, z_lo, y = seq % 2, (seq // 2) % NLO, seq // (2 * NLO)
    z = z_hi * NLO + z_lo
    here = y * NX + x
    sibling = device(x, y, z, 1 - core)
    tokens, width = tok_ref.shape
    depth = gate_ref.shape[1]
    half = depth // 2
    cap = send1.shape[2]
    wide = width // CHUNKS
    rows = rows_in.shape[0]
    group = rows // NY
    per_z = rows // NZ

    own = (
        (tok_hbm, tok_ref), (lengths_hbm, lengths_ref), (routing_hbm, routing_ref),
        (router_hbm, router_ref),
    )
    for n, (src, dst) in enumerate(own):
        copy(src, dst, in_sem.at[n]).start()

    barrier = pltpu.get_barrier_semaphore()

    def greet(to):
        pl.semaphore_signal(barrier, inc=1, device_id=to, device_id_type=MESH)

    @pl.loop(0, NX)
    def _(px):
        greet(device(px, y, z, 1 - core))

    @pl.loop(1, PLANE)
    def _(i):
        at = (here + i) % PLANE
        greet(device(at % NX, at // NX, z, core))

    @pl.loop(1, NZ)
    def _(i):
        greet(device(x, y, (z + i) % NZ, core))

    def send_gate_up(i, m, part):
        ref = (gate_ref, up_ref)[m]
        goal = 2 * core + i
        at = pl.ds(part * half, half)

        @pl.when(goal != x)
        def _():
            push(
                ref.at[i, at, :], gate_up.at[x, m, at, :], g_send, g_recv.at[x],
                device(goal, y, z, part),
            )

        @pl.when(goal == x)
        def _():
            copy(ref.at[i, at, :], gate_up.at[x, m, at, :], g_recv.at[x]).start()
            push(ref.at[i, at, :], gate_up.at[x, m, at, :], g_send, g_recv.at[x], sibling)

    def send_down(i, c, part):
        goal = 2 * core + i
        at, cols = pl.ds(part * half, half), pl.ds(c * wide, wide)

        @pl.when(goal != x)
        def _():
            push(
                down_ref.at[i, at, cols], down.at[x, at, cols], d_send, d_recv.at[x, c],
                device(goal, y, z, part),
            )

        @pl.when(goal == x)
        def _():
            copy(down_ref.at[i, at, cols], down.at[x, at, cols], d_recv.at[x, c]).start()
            push(down_ref.at[i, at, cols], down.at[x, at, cols], d_send, d_recv.at[x, c], sibling)

    for n in range(3):
        copy(*own[n], in_sem.at[n]).wait()
    values = tok_ref[...].astype(f32)
    scale = lax.rsqrt(jnp.mean(values * values, axis=-1, keepdims=True) + 1e-06)
    normed[...] = (values * scale).astype(bf16)
    block = teacher * (2 * NLO * NY) + seq
    first = (block % 4) * tokens
    limit = lengths_ref[block // 4]
    live = first + lax.broadcasted_iota(jnp.int32, (tokens, 1), 0) < limit
    square = (tokens, tokens)
    diagonal = lax.broadcasted_iota(jnp.int32, square, 0) == lax.broadcasted_iota(
        jnp.int32, square, 1
    )

    def upright(row):
        return jnp.sum(jnp.where(diagonal, row, 0), axis=1, keepdims=True)

    name0, name1 = upright(routing_ref[0:1, :]), upright(routing_ref[1:2, :])
    earlier = (
        lax.broadcasted_iota(jnp.int32, square, 0) > lax.broadcasted_iota(jnp.int32, square, 1)
    ).astype(f32).astype(bf16)

    def slots(count, per_place):
        expert, rank = slot_columns((tokens, count), per_place, cap)
        named = jnp.logical_or(name0 == expert, name1 == expert)
        hit = jnp.where(jnp.logical_and(named, live), 1.0, 0.0)
        before = jnp.dot(earlier, hit.astype(bf16), preferred_element_type=f32)
        return expert, jnp.where(before == rank.astype(f32), hit, 0.0)

    _, chosen = slots(PLANE * NLO * cap, NLO * cap)
    picked = lax.dot_general(
        chosen.astype(bf16), normed[...], (((0,), (0,)), ((), ())), preferred_element_type=f32
    )
    for k in range(SUB):
        stage[pl.ds(k, PLANE * NLO * cap, stride=SUB), :] = picked[:, k * LANE:(k + 1) * LANE]
    send1[...] = stage[...].astype(bf16).reshape(send1.shape)

    pl.semaphore_wait(barrier, NX + PLANE - 1 + NZ - 1)
    copy(send1.at[here], plane_in.at[here], p_recv.at[y]).start()

    @pl.loop(1, PLANE)
    def _(i):
        px, py = (x + i) % NX, (y + i // NX) % NY
        push(
            send1.at[py * NX + px], plane_in.at[here], p_send, p_recv.at[y],
            device(px, py, z, core),
        )

    for m in range(2):
        for part in range(2):
            for i in range(2):
                send_gate_up(i, m, part)
    for c in range(CHUNKS):
        for part in range(2):
            for i in range(2):
                send_down(i, c, part)

    copy(*own[3], in_sem.at[3]).wait()
    logits = lax.dot_general(
        normed[...], router_ref[...], (((1,), (1,)), ((), ())), preferred_element_type=f32
    )
    ids = lax.broadcasted_iota(jnp.int32, logits.shape, 1)

    def score(name):
        return jax.nn.sigmoid(
            jnp.sum(jnp.where(name == ids, logits, 0.0), axis=1, keepdims=True)
        )

    score0, score1 = score(name0), score(name1)
    both = score0 + score1
    expert, used = slots(PLANE * SUB, SUB)
    mix = used * jnp.where(name0 == expert, score0 / both, score1 / both)
    high = mix.astype(bf16)
    mix_hi[...] = high
    mix_lo[...] = (mix - high.astype(f32)).astype(bf16)

    @pl.loop(0, NY)
    def _(i):
        g = (y + NY - i) % NY
        at = pl.ds(g * NX, NX)
        take(plane_in.at[at], p_recv.at[g])
        copy(plane_in.at[at, z_lo], recv.at[g, z], z_recv.at[g]).start()

        @pl.loop(1, NZ)
        def _(j):
            pz = (z + j) % NZ
            push(
                plane_in.at[at, pz % NLO], recv.at[g, z], z_send, z_recv.at[g],
                device(x, y, pz, core),
            )

    i_at, q = split(lax.broadcasted_iota(jnp.int32, (rows, rows), 0), per_z)
    by_y, rest = split(q, NX * cap)
    column = lax.broadcasted_iota(jnp.int32, (rows, rows), 1)
    turn = (y + NY - by_y) & (NY - 1)
    order[...] = (turn * group + i_at * (NX * cap) + rest == column).astype(f32).astype(bf16)
    place, left = split(lax.broadcasted_iota(jnp.int32, (PLANE * SUB, rows), 0), SUB)
    from_z, q = split(lax.broadcasted_iota(jnp.int32, (PLANE * SUB, rows), 1), per_z)
    to_place, rank = split(q, cap)
    same = jnp.logical_and(place == to_place, left == (from_z & (NLO - 1)) * cap + rank)
    gather[...] = same.astype(f32).astype(bf16)

    def relayout(i):
        g = (y + NY - i) % NY
        take(recv.at[g], z_recv.at[g])
        part = pl.ds(0, group * SUB)
        stage[part, :] = recv[g].reshape(group * SUB, LANE).astype(f32)
        at = slice(i * group, (i + 1) * group)
        for k in range(SUB):
            rows_in[at, k * LANE:(k + 1) * LANE] = stage[
                pl.ds(k, group, stride=SUB), :
            ].astype(bf16)

    def first_layer(s, at):
        dims = (((1,), (1,)), ((), ()))
        gate = lax.dot_general(rows_in[at, :], gate_up[s, 0], dims, preferred_element_type=f32)
        upper = lax.dot_general(rows_in[at, :], gate_up[s, 1], dims, preferred_element_type=f32)
        hidden[s, at, :] = (gate / (1.0 + jnp.exp(-gate)) * upper).astype(bf16)

    def gate_half(s, part):
        return gate_up.at[s, :, pl.ds(part * half, half), :]

    def down_half(s, c, part):
        return down.at[s, pl.ds(part * half, half), pl.ds(c * wide, wide)]

    relayout(0)
    relayout(1)
    take(gate_up.at[x], g_recv.at[x])
    first_layer(x, slice(0, 2 * group))
    for d in ORDER:
        s = (x + d) % NX
        mine = gate_half(s, core)
        take(mine, g_recv.at[s])
        push(mine, mine, gf_send.at[s], gf_recv.at[s], sibling)
    relayout(2)
    relayout(3)
    first_layer(x, slice(2 * group, 4 * group))
    for d in ORDER:
        s = (x + d) % NX
        take(gate_half(s, 1 - core), gf_recv.at[s])

    @pl.loop(1, NX)
    def _(d):
        first_layer((x + d) % NX, slice(0, rows))

    @pl.loop(0, NX)
    def _(s):
        sorted_hidden[s] = jnp.dot(
            order[...], hidden[s], preferred_element_type=f32
        ).astype(bf16)

    for c in range(CHUNKS):
        for d in ORDER:
            s = (x + d) % NX
            mine = down_half(s, c, core)
            take(mine, d_recv.at[s, c])
            push(mine, mine, df_send.at[s, c], df_recv.at[s, c], sibling)
        cols = pl.ds(c * wide, wide)
        take(down.at[x, :, cols], d_recv.at[x, c])
        for d in ORDER:
            s = (x + d) % NX
            take(down_half(s, c, 1 - core), df_recv.at[s, c])

        @pl.loop(0, rows // 128)
        def _(b):
            at = pl.ds(pl.multiple_of(b * 128, 128), 128)
            total = jnp.zeros((128, wide), f32)
            for s in range(NX):
                total += jnp.dot(
                    sorted_hidden[s, at, :], down[s, :, c * wide:(c + 1) * wide],
                    preferred_element_type=f32,
                )
            rsend[c, at, :] = total.astype(bf16)

        def mine_of(pz):
            return rsend.at[c, pl.ds(pl.multiple_of(pz * per_z, per_z), per_z), :]

        copy(mine_of(z), z_back.at[c, pl.ds(pl.multiple_of(z * per_z, per_z), per_z), :],
             rz_recv.at[c]).start()

        @pl.loop(1, NZ)
        def _(j):
            pz = (z + j) % NZ
            push(
                mine_of(pz),
                z_back.at[c, pl.ds(pl.multiple_of(z * per_z, per_z), per_z), :],
                rz_send, rz_recv.at[c], device(x, y, pz, core),
            )

    def finish(c):
        take(back.at[c], rp_recv.at[c])
        total = jnp.dot(mix_hi[...], back[c], preferred_element_type=f32)
        total += jnp.dot(mix_lo[...], back[c], preferred_element_type=f32)
        out_ref[:, c * wide:(c + 1) * wide] = total.astype(bf16)

    for c in range(CHUNKS):
        take(z_back.at[c], rz_recv.at[c])
        xsend[c] = jnp.dot(gather[...], z_back[c], preferred_element_type=f32).astype(bf16)
        landing = back.at[c, pl.ds(pl.multiple_of(here * SUB, SUB), SUB), :]
        copy(
            xsend.at[c, pl.ds(pl.multiple_of(here * SUB, SUB), SUB), :], landing, rp_recv.at[c]
        ).start()

        @pl.loop(1, PLANE)
        def _(i):
            at = (here + i) % PLANE
            push(
                xsend.at[c, pl.ds(pl.multiple_of(at * SUB, SUB), SUB), :], landing,
                rp_send, rp_recv.at[c], device(at % NX, at // NX, z, core),
            )

        if c > 0:
            finish(c - 1)
    finish(CHUNKS - 1)

    take(plane_in.at[pl.ds(0, PLANE - 1)], p_send)
    take(recv.at[:, pl.ds(0, NZ - 1)], z_send)
    take(z_back.at[:, pl.ds(0, rows - per_z), :], rz_send)
    take(back.at[:, pl.ds(0, (PLANE - 1) * SUB), :], rp_send)
    take(gate_up.at[pl.ds(0, 2)], g_send)
    take(down.at[pl.ds(0, 2)], d_send)
    for d in ORDER:
        s = (x + d) % NX
        take(gate_half(s, core), gf_send.at[s])
        for c in range(CHUNKS):
            take(down_half(s, c, core), df_send.at[s, c])


def local(tokens, router_weight, gate_weight, up_weight, down_weight, routing, lengths):
    tok_dev, width = tokens.shape
    top_count = routing.shape[1]
    experts = gate_weight.shape[0] * lax.axis_size("seq")
    depth = gate_weight.shape[1]
    cap = max(2, tok_dev * top_count // experts + 1)
    rows = PLANE * NZ * cap
    wide = width // CHUNKS
    vmem = pl.BlockSpec(memory_space=pltpu.VMEM)
    hbm = pl.BlockSpec(memory_space=pltpu.HBM)
    sem = pltpu.SemaphoreType.DMA
    bf16 = jnp.bfloat16
    return pl.pallas_call(
        kernel,
        out_shape=jax.ShapeDtypeStruct((tok_dev, width), bf16),
        in_specs=[hbm] * 7,
        out_specs=vmem,
        scratch_shapes=[
            pltpu.SMEM(lengths.shape, jnp.int32),
            pltpu.VMEM((tok_dev, width), bf16),
            pltpu.VMEM((experts, width), bf16),
            pltpu.VMEM((top_count, tok_dev), jnp.int32),
            pltpu.VMEM((tok_dev, width), bf16),
            pltpu.VMEM((tok_dev, PLANE * SUB), bf16),
            pltpu.VMEM((tok_dev, PLANE * SUB), bf16),
            pltpu.VMEM((rows, rows), bf16),
            pltpu.VMEM((PLANE * SUB, rows), bf16),
            pltpu.VMEM((PLANE, NLO, cap, SUB, LANE), bf16),
            pltpu.VMEM((PLANE, NLO, cap, SUB, LANE), bf16),
            pltpu.VMEM((NY, NZ, NX, cap, SUB, LANE), bf16),
            pltpu.VMEM((rows, width), bf16),
            pltpu.VMEM((NX, 2, depth, width), bf16),
            pltpu.VMEM((NX, depth, width), bf16),
            pltpu.VMEM((NX, rows, depth), bf16),
            pltpu.VMEM((NX, rows, depth), bf16),
            pltpu.VMEM((PLANE * NLO * cap * SUB, LANE), jnp.float32),
            pltpu.VMEM((CHUNKS, rows, wide), bf16),
            pltpu.VMEM((CHUNKS, rows, wide), bf16),
            pltpu.VMEM((CHUNKS, PLANE * SUB, wide), bf16),
            pltpu.VMEM((CHUNKS, PLANE * SUB, wide), bf16),
            sem, sem((NX,)), sem((NX,)), sem((NX,)),
            sem, sem((NX, CHUNKS)), sem((NX, CHUNKS)), sem((NX, CHUNKS)),
            sem, sem((NY,)), sem, sem((NY,)),
            sem, sem((CHUNKS,)), sem, sem((CHUNKS,)), sem((4,)),
        ],
        compiler_params=pltpu.CompilerParams(
            collective_id=0, has_side_effects=True, vmem_limit_bytes=60 * 1024 * 1024
        ),
    )(lengths, tokens, router_weight.T, routing.T, gate_weight, up_weight, down_weight)


def solution(mesh):
    in_specs = (
        P(("teacher", "seq"), None),
        P(),
        P("seq", "teacher", None),
        P("seq", "teacher", None),
        P("seq", "teacher", None),
        P(("teacher", "seq"), None),
        P(),
    )
    out_specs = P(("teacher", "seq"), None)
    return jax.shard_map(local, mesh=mesh, in_specs=in_specs, out_specs=out_specs, check_vma=False)
```

```python
import jax
import jax.numpy as jnp
from jax import lax
from jax.experimental import pallas as pl
from jax.experimental.pallas import tpu as pltpu
from jax.sharding import PartitionSpec as P

MESH = pl.DeviceIdType.MESH
NX, NY, NZ, NLO = 4, 4, 8, 4
PLANE = NX * NY
LANE = 128
SUB = 16
CHUNKS = 8
ORDER = (1, 3, 2)
LAG = 2
PIECES = ((0, 0, 2), (1, 0, 1), (1, 1, 1))


def device(x, y, z, core):
    return ((z // NLO) * NX + x, (y * NLO + z % NLO) * 2 + core)


def split(values, by):
    if by == 16:
        whole = lax.shift_right_logical(values, 4)
    else:
        whole = lax.shift_right_logical(values * 171, {3: 9, 12: 11, 48: 13}[by])
    return whole, values - whole * by


def slot_columns(shape, per_place, cap):
    place, left = split(lax.broadcasted_iota(jnp.int32, shape, 1), per_place)
    z_lo, rank = split(left, cap)
    y, x = lax.shift_right_logical(place, 2), place & (NX - 1)
    expert = jnp.where(left < NLO * cap, (y * NLO + z_lo) * NX + x, -1)
    return expert, rank


def copy(src, dst, sem):
    return pltpu.make_async_copy(src, dst, sem)


def push(src, dst, send_sem, recv_sem, to):
    pltpu.make_async_remote_copy(
        src_ref=src, dst_ref=dst, send_sem=send_sem, recv_sem=recv_sem,
        device_id=to, device_id_type=MESH,
    ).start()


def take(ref, sem):
    pltpu.make_async_copy(ref, ref, sem).wait()


def kernel(
    lengths_hbm, tok_hbm, router_hbm, routing_hbm, gate_ref, up_ref, down_ref, out_ref,
    lengths_ref, tok_ref, router_ref, routing_ref, normed, mix_hi, mix_lo, order, gather, send1, plane_in, recv, rows_in, gate_up, down,
    gates, hidden, sorted_hidden, stage, rsend, z_back, xsend, back,
    g_send, g_recv, gf_send, gf_recv, d_send, d_recv, df_send, df_recv,
    p_send, p_recv, z_send, z_recv, rz_send, rz_recv, rp_send, rp_recv, in_sem,
):
    f32, bf16 = jnp.float32, jnp.bfloat16
    teacher, seq = lax.axis_index("teacher"), lax.axis_index("seq")
    x, z_hi = teacher % NX, teacher // NX
    core, z_lo, y = seq % 2, (seq // 2) % NLO, seq // (2 * NLO)
    z = z_hi * NLO + z_lo
    here = y * NX + x
    sibling = device(x, y, z, 1 - core)
    tokens, width = tok_ref.shape
    depth = gate_ref.shape[1]
    half = depth // 2
    cap = send1.shape[2]
    wide = width // CHUNKS
    rows = rows_in.shape[0]
    group = rows // NY
    per_z = rows // NZ

    own = (
        (tok_hbm, tok_ref), (lengths_hbm, lengths_ref), (routing_hbm, routing_ref),
        (router_hbm, router_ref),
    )
    for n, (src, dst) in enumerate(own):
        copy(src, dst, in_sem.at[n]).start()

    barrier = pltpu.get_barrier_semaphore()

    def greet(to):
        pl.semaphore_signal(barrier, inc=1, device_id=to, device_id_type=MESH)

    @pl.loop(1, NZ)
    def _(i):
        greet(device(x, y, (z + i) % NZ, core))

    @pl.loop(1, PLANE)
    def _(i):
        at = (here + i) % PLANE
        greet(device(at % NX, at // NX, z, core))

    @pl.loop(0, NX)
    def _(px):
        greet(device(px, y, z, 1 - core))

    def piece(p, part):
        m, start, count = PIECES[p]
        return m, pl.ds(part * half + start * (half // 2), count * (half // 2))

    def send_gate_up(i, p, part):
        m, at = piece(p, part)
        src = (gate_ref, up_ref)[m].at[i, at, :]
        dst = gate_up.at[x, m, at, :]
        goal = 2 * core + i

        @pl.when(goal != x)
        def _():
            push(src, dst, g_send, g_recv.at[x, p], device(goal, y, z, part))

        @pl.when(goal == x)
        def _():
            copy(src, dst, g_recv.at[x, p]).start()
            push(src, dst, g_send, g_recv.at[x, p], sibling)

    def send_down(i, c, part):
        goal = 2 * core + i
        at, cols = pl.ds(part * half, half), pl.ds(c * wide, wide)

        @pl.when(goal != x)
        def _():
            push(
                down_ref.at[i, at, cols], down.at[x, at, cols], d_send, d_recv.at[x, c],
                device(goal, y, z, part),
            )

        @pl.when(goal == x)
        def _():
            copy(down_ref.at[i, at, cols], down.at[x, at, cols], d_recv.at[x, c]).start()
            push(down_ref.at[i, at, cols], down.at[x, at, cols], d_send, d_recv.at[x, c], sibling)

    for n in range(3):
        copy(*own[n], in_sem.at[n]).wait()
    values = tok_ref[...].astype(f32)
    scale = lax.rsqrt(jnp.mean(values * values, axis=-1, keepdims=True) + 1e-06)
    normed[...] = (values * scale).astype(bf16)

    pl.semaphore_wait(barrier, NX + PLANE - 1 + NZ - 1)
    block = teacher * (2 * NLO * NY) + seq
    first = (block % 4) * tokens
    limit = lengths_ref[block // 4]
    live = first + lax.broadcasted_iota(jnp.int32, (tokens, 1), 0) < limit
    square = (tokens, tokens)
    diagonal = lax.broadcasted_iota(jnp.int32, square, 0) == lax.broadcasted_iota(
        jnp.int32, square, 1
    )

    def upright(row):
        return jnp.sum(jnp.where(diagonal, row, 0), axis=1, keepdims=True)

    name0, name1 = upright(routing_ref[0:1, :]), upright(routing_ref[1:2, :])
    earlier = (
        lax.broadcasted_iota(jnp.int32, square, 0) > lax.broadcasted_iota(jnp.int32, square, 1)
    ).astype(f32).astype(bf16)

    def slots(count, per_place):
        expert, rank = slot_columns((tokens, count), per_place, cap)
        named = jnp.logical_or(name0 == expert, name1 == expert)
        hit = jnp.where(jnp.logical_and(named, live), 1.0, 0.0)
        before = jnp.dot(earlier, hit.astype(bf16), preferred_element_type=f32)
        return expert, jnp.where(before == rank.astype(f32), hit, 0.0)

    _, chosen = slots(PLANE * NLO * cap, NLO * cap)
    picked = lax.dot_general(
        chosen.astype(bf16), normed[...], (((0,), (0,)), ((), ())), preferred_element_type=f32
    )
    for k in range(SUB):
        stage[pl.ds(k, PLANE * NLO * cap, stride=SUB), :] = picked[:, k * LANE:(k + 1) * LANE]
    send1[...] = stage[...].astype(bf16).reshape(send1.shape)

    copy(send1.at[here], plane_in.at[here], p_recv.at[y]).start()

    @pl.loop(1, PLANE)
    def _(i):
        px, py = (x + i) % NX, (y + i // NX) % NY
        push(
            send1.at[py * NX + px], plane_in.at[here], p_send, p_recv.at[y],
            device(px, py, z, core),
        )

    for p in range(len(PIECES)):
        for part in range(2):
            for i in range(2):
                send_gate_up(i, p, part)
    for c in range(CHUNKS):
        for part in range(2):
            for i in range(2):
                send_down(i, c, part)

    copy(*own[3], in_sem.at[3]).wait()
    logits = lax.dot_general(
        normed[...], router_ref[...], (((1,), (1,)), ((), ())), preferred_element_type=f32
    )
    ids = lax.broadcasted_iota(jnp.int32, logits.shape, 1)

    def score(name):
        return jax.nn.sigmoid(
            jnp.sum(jnp.where(name == ids, logits, 0.0), axis=1, keepdims=True)
        )

    score0, score1 = score(name0), score(name1)
    both = score0 + score1
    expert, used = slots(PLANE * SUB, SUB)
    mix = used * jnp.where(name0 == expert, score0 / both, score1 / both)
    high = mix.astype(bf16)
    mix_hi[...] = high
    mix_lo[...] = (mix - high.astype(f32)).astype(bf16)

    @pl.loop(0, NY)
    def _(i):
        g = (y + NY - i) % NY
        at = pl.ds(g * NX, NX)
        take(plane_in.at[at], p_recv.at[g])
        copy(plane_in.at[at, z_lo], recv.at[g, z], z_recv.at[g]).start()

        @pl.loop(1, NZ)
        def _(j):
            pz = (z + NZ // 2 + (1 - 2 * (j % 2)) * (j // 2)) % NZ
            push(
                plane_in.at[at, pz % NLO], recv.at[g, z], z_send, z_recv.at[g],
                device(x, y, pz, core),
            )

    i_at, q = split(lax.broadcasted_iota(jnp.int32, (rows, rows), 0), per_z)
    by_y, rest = split(q, NX * cap)
    column = lax.broadcasted_iota(jnp.int32, (rows, rows), 1)
    turn = (y + NY - by_y) & (NY - 1)
    order[...] = (turn * group + i_at * (NX * cap) + rest == column).astype(f32).astype(bf16)
    place, left = split(lax.broadcasted_iota(jnp.int32, (PLANE * SUB, rows), 0), SUB)
    from_z, q = split(lax.broadcasted_iota(jnp.int32, (PLANE * SUB, rows), 1), per_z)
    to_place, rank = split(q, cap)
    same = jnp.logical_and(place == to_place, left == (from_z & (NLO - 1)) * cap + rank)
    gather[...] = same.astype(f32).astype(bf16)

    def relayout(i):
        g = (y + NY - i) % NY
        take(recv.at[g], z_recv.at[g])
        part = pl.ds(0, group * SUB)
        stage[part, :] = recv[g].reshape(group * SUB, LANE).astype(f32)
        at = slice(i * group, (i + 1) * group)
        for k in range(SUB):
            rows_in[at, k * LANE:(k + 1) * LANE] = stage[
                pl.ds(k, group, stride=SUB), :
            ].astype(bf16)

    def times(s, m, at):
        return lax.dot_general(
            rows_in[at, :], gate_up[s, m], (((1,), (1,)), ((), ())), preferred_element_type=f32
        )

    def first_gate(s, at):
        gates[s, at, :] = times(s, 0, at)

    def first_up(s, at):
        gate = gates[s, at, :]
        hidden[s, at, :] = (gate / (1.0 + jnp.exp(-gate)) * times(s, 1, at)).astype(bf16)

    def sort(s):
        sorted_hidden[s] = jnp.dot(
            order[...], hidden[s], preferred_element_type=f32
        ).astype(bf16)

    def down_half(s, c, part):
        return down.at[s, pl.ds(part * half, half), pl.ds(c * wide, wide)]

    def landed(s, p, part):
        m, at = piece(p, part)
        return gate_up.at[s, m, at, :]

    def forward(p):
        for d in ORDER:
            s = (x + d) % NX
            mine = landed(s, p, core)
            take(mine, g_recv.at[s, p])
            push(mine, mine, gf_send.at[s, p], gf_recv.at[s, p], sibling)

    def forwarded(p):
        for d in ORDER:
            s = (x + d) % NX
            take(landed(s, p, 1 - core), gf_recv.at[s, p])

    early, late, every = slice(0, 2 * group), slice(2 * group, 4 * group), slice(0, rows)
    for p, (m, _, count) in enumerate(PIECES):
        take(gate_up.at[x, m, pl.ds(0, count * half), :], g_recv.at[x, p])
    relayout(0)
    relayout(1)
    first_gate(x, early)
    first_up(x, early)
    forward(0)
    forwarded(0)

    @pl.loop(1, NX)
    def _(d):
        first_gate((x + d) % NX, early)

    forward(1)
    relayout(2)
    relayout(3)
    first_gate(x, late)
    first_up(x, late)
    sort(x)

    @pl.loop(1, NX)
    def _(d):
        first_gate((x + d) % NX, late)

    forward(2)
    forwarded(1)
    forwarded(2)

    @pl.loop(1, NX)
    def _(d):
        s = (x + d) % NX
        first_up(s, every)
        sort(s)

    for c in range(CHUNKS):
        for d in ORDER:
            s = (x + d) % NX
            mine = down_half(s, c, core)
            take(mine, d_recv.at[s, c])
            push(mine, mine, df_send.at[s, c], df_recv.at[s, c], sibling)
        cols = pl.ds(c * wide, wide)
        take(down.at[x, :, cols], d_recv.at[x, c])
        for d in ORDER:
            s = (x + d) % NX
            take(down_half(s, c, 1 - core), df_recv.at[s, c])

        @pl.loop(0, rows // 128)
        def _(b):
            at = pl.ds(pl.multiple_of(b * 128, 128), 128)
            total = jnp.zeros((128, wide), f32)
            for s in range(NX):
                total += jnp.dot(
                    sorted_hidden[s, at, :], down[s, :, c * wide:(c + 1) * wide],
                    preferred_element_type=f32,
                )
            rsend[c, at, :] = total.astype(bf16)

        def mine_of(pz):
            return rsend.at[c, pl.ds(pl.multiple_of(pz * per_z, per_z), per_z), :]

        copy(mine_of(z), z_back.at[c, pl.ds(pl.multiple_of(z * per_z, per_z), per_z), :],
             rz_recv.at[c]).start()

        @pl.loop(1, NZ)
        def _(j):
            pz = (z + NZ // 2 + (1 - 2 * (j % 2)) * (j // 2)) % NZ
            push(
                mine_of(pz),
                z_back.at[c, pl.ds(pl.multiple_of(z * per_z, per_z), per_z), :],
                rz_send, rz_recv.at[c], device(x, y, pz, core),
            )

    def finish(c):
        take(back.at[c], rp_recv.at[c])
        total = jnp.dot(mix_hi[...], back[c], preferred_element_type=f32)
        total += jnp.dot(mix_lo[...], back[c], preferred_element_type=f32)
        out_ref[:, c * wide:(c + 1) * wide] = total.astype(bf16)

    for c in range(CHUNKS):
        take(z_back.at[c], rz_recv.at[c])
        xsend[c] = jnp.dot(gather[...], z_back[c], preferred_element_type=f32).astype(bf16)
        landing = back.at[c, pl.ds(pl.multiple_of(here * SUB, SUB), SUB), :]
        copy(
            xsend.at[c, pl.ds(pl.multiple_of(here * SUB, SUB), SUB), :], landing, rp_recv.at[c]
        ).start()

        @pl.loop(1, PLANE)
        def _(i):
            at = (here + i) % PLANE
            push(
                xsend.at[c, pl.ds(pl.multiple_of(at * SUB, SUB), SUB), :], landing,
                rp_send, rp_recv.at[c], device(at % NX, at // NX, z, core),
            )

        if c >= LAG:
            finish(c - LAG)
    for c in range(CHUNKS - LAG, CHUNKS):
        finish(c)

    take(plane_in.at[pl.ds(0, PLANE - 1)], p_send)
    take(recv.at[:, pl.ds(0, NZ - 1)], z_send)
    take(z_back.at[:, pl.ds(0, rows - per_z), :], rz_send)
    take(back.at[:, pl.ds(0, (PLANE - 1) * SUB), :], rp_send)
    take(gate_up.at[pl.ds(0, 2)], g_send)
    take(down.at[pl.ds(0, 2)], d_send)
    for d in ORDER:
        s = (x + d) % NX
        for p in range(len(PIECES)):
            take(landed(s, p, core), gf_send.at[s, p])
        for c in range(CHUNKS):
            take(down_half(s, c, core), df_send.at[s, c])


def local(tokens, router_weight, gate_weight, up_weight, down_weight, routing, lengths):
    tok_dev, width = tokens.shape
    top_count = routing.shape[1]
    experts = gate_weight.shape[0] * lax.axis_size("seq")
    depth = gate_weight.shape[1]
    cap = max(2, tok_dev * top_count // experts + 1)
    rows = PLANE * NZ * cap
    wide = width // CHUNKS
    vmem = pl.BlockSpec(memory_space=pltpu.VMEM)
    hbm = pl.BlockSpec(memory_space=pltpu.HBM)
    sem = pltpu.SemaphoreType.DMA
    bf16 = jnp.bfloat16
    return pl.pallas_call(
        kernel,
        out_shape=jax.ShapeDtypeStruct((tok_dev, width), bf16),
        in_specs=[hbm] * 7,
        out_specs=vmem,
        scratch_shapes=[
            pltpu.SMEM(lengths.shape, jnp.int32),
            pltpu.VMEM((tok_dev, width), bf16),
            pltpu.VMEM((experts, width), bf16),
            pltpu.VMEM((top_count, tok_dev), jnp.int32),
            pltpu.VMEM((tok_dev, width), bf16),
            pltpu.VMEM((tok_dev, PLANE * SUB), bf16),
            pltpu.VMEM((tok_dev, PLANE * SUB), bf16),
            pltpu.VMEM((rows, rows), bf16),
            pltpu.VMEM((PLANE * SUB, rows), bf16),
            pltpu.VMEM((PLANE, NLO, cap, SUB, LANE), bf16),
            pltpu.VMEM((PLANE, NLO, cap, SUB, LANE), bf16),
            pltpu.VMEM((NY, NZ, NX, cap, SUB, LANE), bf16),
            pltpu.VMEM((rows, width), bf16),
            pltpu.VMEM((NX, 2, depth, width), bf16),
            pltpu.VMEM((NX, depth, width), bf16),
            pltpu.VMEM((NX, rows, depth), jnp.float32),
            pltpu.VMEM((NX, rows, depth), bf16),
            pltpu.VMEM((NX, rows, depth), bf16),
            pltpu.VMEM((PLANE * NLO * cap * SUB, LANE), jnp.float32),
            pltpu.VMEM((CHUNKS, rows, wide), bf16),
            pltpu.VMEM((CHUNKS, rows, wide), bf16),
            pltpu.VMEM((CHUNKS, PLANE * SUB, wide), bf16),
            pltpu.VMEM((CHUNKS, PLANE * SUB, wide), bf16),
            sem, *[sem((NX, len(PIECES)))] * 3,
            sem, sem((NX, CHUNKS)), sem((NX, CHUNKS)), sem((NX, CHUNKS)),
            sem, sem((NY,)), sem, sem((NY,)),
            sem, sem((CHUNKS,)), sem, sem((CHUNKS,)), sem((4,)),
        ],
        compiler_params=pltpu.CompilerParams(
            collective_id=0, has_side_effects=True, vmem_limit_bytes=60 * 1024 * 1024
        ),
    )(lengths, tokens, router_weight.T, routing.T, gate_weight, up_weight, down_weight)


def solution(mesh):
    in_specs = (
        P(("teacher", "seq"), None),
        P(),
        P("seq", "teacher", None),
        P("seq", "teacher", None),
        P("seq", "teacher", None),
        P(("teacher", "seq"), None),
        P(),
    )
    out_specs = P(("teacher", "seq"), None)
    return jax.shard_map(local, mesh=mesh, in_specs=in_specs, out_specs=out_specs, check_vma=False)
```

```python
import jax
import jax.numpy as jnp
from jax import lax
from jax.experimental import pallas as pl
from jax.experimental.pallas import tpu as pltpu
from jax.sharding import PartitionSpec as P

MESH = pl.DeviceIdType.MESH
NX, NY, NZ, NLO = 4, 4, 8, 4
PLANE = NX * NY
LANE = 128
SUB = 16
CHUNKS = 8
ORDER = (1, 3, 2)
LAG = 2
BEFORE = 2
PIECES = ((0, 0, 2), (1, 0, 1), (1, 1, 1))


def device(x, y, z, core):
    return ((z // NLO) * NX + x, (y * NLO + z % NLO) * 2 + core)


def split(values, by):
    if by == 16:
        whole = lax.shift_right_logical(values, 4)
    else:
        whole = lax.shift_right_logical(values * 171, {3: 9, 12: 11, 48: 13}[by])
    return whole, values - whole * by


def slot_columns(shape, per_place, cap):
    place, left = split(lax.broadcasted_iota(jnp.int32, shape, 1), per_place)
    z_lo, rank = split(left, cap)
    y, x = lax.shift_right_logical(place, 2), place & (NX - 1)
    expert = jnp.where(left < NLO * cap, (y * NLO + z_lo) * NX + x, -1)
    return expert, rank


def copy(src, dst, sem):
    return pltpu.make_async_copy(src, dst, sem)


def push(src, dst, send_sem, recv_sem, to):
    pltpu.make_async_remote_copy(
        src_ref=src, dst_ref=dst, send_sem=send_sem, recv_sem=recv_sem,
        device_id=to, device_id_type=MESH,
    ).start()


def take(ref, sem):
    pltpu.make_async_copy(ref, ref, sem).wait()


def kernel(
    lengths_hbm, tok_hbm, router_hbm, routing_hbm, gate_ref, up_ref, down_ref, out_ref,
    lengths_ref, tok_ref, router_ref, routing_ref, normed, mix_hi, mix_lo, order, gather, send1, plane_in, recv, rows_in, gate_up, down,
    gates, hidden, sorted_hidden, stage, rsend, z_back, xsend, back,
    g_send, g_recv, gf_send, gf_recv, d_send, d_recv, df_send, df_recv,
    p_send, p_recv, z_send, z_recv, rz_send, rz_recv, rp_send, rp_recv, in_sem,
):
    f32, bf16 = jnp.float32, jnp.bfloat16
    teacher, seq = lax.axis_index("teacher"), lax.axis_index("seq")
    x, z_hi = teacher % NX, teacher // NX
    core, z_lo, y = seq % 2, (seq // 2) % NLO, seq // (2 * NLO)
    z = z_hi * NLO + z_lo
    here = y * NX + x
    sibling = device(x, y, z, 1 - core)
    tokens, width = tok_ref.shape
    depth = gate_ref.shape[1]
    half = depth // 2
    cap = send1.shape[2]
    wide = width // CHUNKS
    rows = rows_in.shape[0]
    group = rows // NY
    per_z = rows // NZ

    own = (
        (tok_hbm, tok_ref), (lengths_hbm, lengths_ref), (routing_hbm, routing_ref),
        (router_hbm, router_ref),
    )
    for n, (src, dst) in enumerate(own):
        copy(src, dst, in_sem.at[n]).start()

    barrier = pltpu.get_barrier_semaphore()

    def greet(to):
        pl.semaphore_signal(barrier, inc=1, device_id=to, device_id_type=MESH)

    @pl.loop(1, NZ)
    def _(i):
        greet(device(x, y, (z + i) % NZ, core))

    @pl.loop(1, PLANE)
    def _(i):
        at = (here + i) % PLANE
        greet(device(at % NX, at // NX, z, core))

    @pl.loop(0, NX)
    def _(px):
        greet(device(px, y, z, 1 - core))

    def piece(p, part):
        m, start, count = PIECES[p]
        return m, pl.ds(part * half + start * (half // 2), count * (half // 2))

    def send_gate_up(i, p, part):
        m, at = piece(p, part)
        src = (gate_ref, up_ref)[m].at[i, at, :]
        dst = gate_up.at[x, m, at, :]
        goal = 2 * core + i

        @pl.when(goal != x)
        def _():
            push(src, dst, g_send, g_recv.at[x, p], device(goal, y, z, part))

        @pl.when(goal == x)
        def _():
            copy(src, dst, g_recv.at[x, p]).start()
            push(src, dst, g_send, g_recv.at[x, p], sibling)

    def send_down(i, c, part):
        goal = 2 * core + i
        at, cols = pl.ds(part * half, half), pl.ds(c * wide, wide)

        @pl.when(goal != x)
        def _():
            push(
                down_ref.at[i, at, cols], down.at[x, at, cols], d_send, d_recv.at[x, c],
                device(goal, y, z, part),
            )

        @pl.when(goal == x)
        def _():
            copy(down_ref.at[i, at, cols], down.at[x, at, cols], d_recv.at[x, c]).start()
            push(down_ref.at[i, at, cols], down.at[x, at, cols], d_send, d_recv.at[x, c], sibling)

    for n in range(3):
        copy(*own[n], in_sem.at[n]).wait()
    values = tok_ref[...].astype(f32)
    scale = lax.rsqrt(jnp.mean(values * values, axis=-1, keepdims=True) + 1e-06)
    normed[...] = (values * scale).astype(bf16)

    pl.semaphore_wait(barrier, NX + PLANE - 1 + NZ - 1)
    block = teacher * (2 * NLO * NY) + seq
    first = (block % 4) * tokens
    limit = lengths_ref[block // 4]
    live = first + lax.broadcasted_iota(jnp.int32, (tokens, 1), 0) < limit
    square = (tokens, tokens)
    diagonal = lax.broadcasted_iota(jnp.int32, square, 0) == lax.broadcasted_iota(
        jnp.int32, square, 1
    )

    def upright(row):
        return jnp.sum(jnp.where(diagonal, row, 0), axis=1, keepdims=True)

    name0, name1 = upright(routing_ref[0:1, :]), upright(routing_ref[1:2, :])
    earlier = (
        lax.broadcasted_iota(jnp.int32, square, 0) > lax.broadcasted_iota(jnp.int32, square, 1)
    ).astype(f32).astype(bf16)

    def slots(count, per_place):
        expert, rank = slot_columns((tokens, count), per_place, cap)
        named = jnp.logical_or(name0 == expert, name1 == expert)
        hit = jnp.where(jnp.logical_and(named, live), 1.0, 0.0)
        before = jnp.dot(earlier, hit.astype(bf16), preferred_element_type=f32)
        return expert, jnp.where(before == rank.astype(f32), hit, 0.0)

    _, chosen = slots(PLANE * NLO * cap, NLO * cap)
    picked = lax.dot_general(
        chosen.astype(bf16), normed[...], (((0,), (0,)), ((), ())), preferred_element_type=f32
    )
    for k in range(SUB):
        stage[pl.ds(k, PLANE * NLO * cap, stride=SUB), :] = picked[:, k * LANE:(k + 1) * LANE]
    send1[...] = stage[...].astype(bf16).reshape(send1.shape)

    copy(send1.at[here], plane_in.at[here], p_recv.at[y]).start()

    @pl.loop(1, PLANE)
    def _(i):
        px, py = (x + i) % NX, (y + i // NX) % NY
        push(
            send1.at[py * NX + px], plane_in.at[here], p_send, p_recv.at[y],
            device(px, py, z, core),
        )

    for p in range(len(PIECES)):
        for part in range(2):
            for i in range(2):
                send_gate_up(i, p, part)
    @pl.loop(0, NY)
    def _(i):
        g = (y + NY - i) % NY
        at = pl.ds(g * NX, NX)
        take(plane_in.at[at], p_recv.at[g])
        copy(plane_in.at[at, z_lo], recv.at[g, z], z_recv.at[g]).start()

        @pl.loop(1, NZ)
        def _(j):
            pz = (z + NZ // 2 + (1 - 2 * (j % 2)) * (j // 2)) % NZ
            push(
                plane_in.at[at, pz % NLO], recv.at[g, z], z_send, z_recv.at[g],
                device(x, y, pz, core),
            )

    for c in range(CHUNKS):
        for part in range(2):
            for i in range(2):
                send_down(i, c, part)

    copy(*own[3], in_sem.at[3]).wait()
    logits = lax.dot_general(
        normed[...], router_ref[...], (((1,), (1,)), ((), ())), preferred_element_type=f32
    )
    ids = lax.broadcasted_iota(jnp.int32, logits.shape, 1)

    def score(name):
        return jax.nn.sigmoid(
            jnp.sum(jnp.where(name == ids, logits, 0.0), axis=1, keepdims=True)
        )

    score0, score1 = score(name0), score(name1)
    both = score0 + score1
    expert, used = slots(PLANE * SUB, SUB)
    mix = used * jnp.where(name0 == expert, score0 / both, score1 / both)
    high = mix.astype(bf16)
    mix_hi[...] = high
    mix_lo[...] = (mix - high.astype(f32)).astype(bf16)

    i_at, q = split(lax.broadcasted_iota(jnp.int32, (rows, rows), 0), per_z)
    by_y, rest = split(q, NX * cap)
    column = lax.broadcasted_iota(jnp.int32, (rows, rows), 1)
    turn = (y + NY - by_y) & (NY - 1)
    order[...] = (turn * group + i_at * (NX * cap) + rest == column).astype(f32).astype(bf16)
    place, left = split(lax.broadcasted_iota(jnp.int32, (PLANE * SUB, rows), 0), SUB)
    from_z, q = split(lax.broadcasted_iota(jnp.int32, (PLANE * SUB, rows), 1), per_z)
    to_place, rank = split(q, cap)
    same = jnp.logical_and(place == to_place, left == (from_z & (NLO - 1)) * cap + rank)
    gather[...] = same.astype(f32).astype(bf16)

    def relayout(i):
        g = (y + NY - i) % NY
        take(recv.at[g], z_recv.at[g])
        part = pl.ds(0, group * SUB)
        stage[part, :] = recv[g].reshape(group * SUB, LANE).astype(f32)
        at = slice(i * group, (i + 1) * group)
        for k in range(SUB):
            rows_in[at, k * LANE:(k + 1) * LANE] = stage[
                pl.ds(k, group, stride=SUB), :
            ].astype(bf16)

    def times(s, m, at):
        return lax.dot_general(
            rows_in[at, :], gate_up[s, m], (((1,), (1,)), ((), ())), preferred_element_type=f32
        )

    def first_gate(s, at):
        gates[s, at, :] = times(s, 0, at)

    def first_up(s, at):
        gate = gates[s, at, :]
        hidden[s, at, :] = (gate / (1.0 + jnp.exp(-gate)) * times(s, 1, at)).astype(bf16)

    def sort(s):
        sorted_hidden[s] = jnp.dot(
            order[...], hidden[s], preferred_element_type=f32
        ).astype(bf16)

    def down_half(s, c, part):
        return down.at[s, pl.ds(part * half, half), pl.ds(c * wide, wide)]

    def landed(s, p, part):
        m, at = piece(p, part)
        return gate_up.at[s, m, at, :]

    def forward(p):
        for d in ORDER:
            s = (x + d) % NX
            mine = landed(s, p, core)
            take(mine, g_recv.at[s, p])
            push(mine, mine, gf_send.at[s, p], gf_recv.at[s, p], sibling)

    def forwarded(p):
        for d in ORDER:
            s = (x + d) % NX
            take(landed(s, p, 1 - core), gf_recv.at[s, p])

    early, late, every = slice(0, 2 * group), slice(2 * group, 4 * group), slice(0, rows)
    for p, (m, _, count) in enumerate(PIECES):
        take(gate_up.at[x, m, pl.ds(0, count * half), :], g_recv.at[x, p])
    relayout(0)
    relayout(1)
    first_gate(x, early)
    first_up(x, early)
    forward(0)
    forwarded(0)

    @pl.loop(1, NX)
    def _(d):
        first_gate((x + d) % NX, early)

    forward(1)
    relayout(2)
    relayout(3)
    first_gate(x, late)
    first_up(x, late)
    sort(x)

    @pl.loop(1, NX)
    def _(d):
        first_gate((x + d) % NX, late)

    forward(2)
    forwarded(1)
    forwarded(2)

    def last_up(d):
        s = (x + d) % NX
        first_up(s, every)
        sort(s)

    def forward_down(c):
        for d in ORDER:
            s = (x + d) % NX
            mine = down_half(s, c, core)
            take(mine, d_recv.at[s, c])
            push(mine, mine, df_send.at[s, c], df_recv.at[s, c], sibling)

    pl.loop(1, BEFORE)(last_up)
    forward_down(0)
    pl.loop(BEFORE, NX)(last_up)

    for c in range(CHUNKS):
        if c > 0:
            forward_down(c)
        cols = pl.ds(c * wide, wide)
        take(down.at[x, :, cols], d_recv.at[x, c])
        for d in ORDER:
            s = (x + d) % NX
            take(down_half(s, c, 1 - core), df_recv.at[s, c])

        @pl.loop(0, rows // 128)
        def _(b):
            at = pl.ds(pl.multiple_of(b * 128, 128), 128)
            total = jnp.zeros((128, wide), f32)
            for s in range(NX):
                total += jnp.dot(
                    sorted_hidden[s, at, :], down[s, :, c * wide:(c + 1) * wide],
                    preferred_element_type=f32,
                )
            rsend[c, at, :] = total.astype(bf16)

        def mine_of(pz):
            return rsend.at[c, pl.ds(pl.multiple_of(pz * per_z, per_z), per_z), :]

        copy(mine_of(z), z_back.at[c, pl.ds(pl.multiple_of(z * per_z, per_z), per_z), :],
             rz_recv.at[c]).start()

        @pl.loop(1, NZ)
        def _(j):
            pz = (z + NZ // 2 + (1 - 2 * (j % 2)) * (j // 2)) % NZ
            push(
                mine_of(pz),
                z_back.at[c, pl.ds(pl.multiple_of(z * per_z, per_z), per_z), :],
                rz_send, rz_recv.at[c], device(x, y, pz, core),
            )

    def finish(c):
        take(back.at[c], rp_recv.at[c])
        total = jnp.dot(mix_hi[...], back[c], preferred_element_type=f32)
        total += jnp.dot(mix_lo[...], back[c], preferred_element_type=f32)
        out_ref[:, c * wide:(c + 1) * wide] = total.astype(bf16)

    for c in range(CHUNKS):
        take(z_back.at[c], rz_recv.at[c])
        xsend[c] = jnp.dot(gather[...], z_back[c], preferred_element_type=f32).astype(bf16)
        landing = back.at[c, pl.ds(pl.multiple_of(here * SUB, SUB), SUB), :]
        copy(
            xsend.at[c, pl.ds(pl.multiple_of(here * SUB, SUB), SUB), :], landing, rp_recv.at[c]
        ).start()

        @pl.loop(1, PLANE)
        def _(i):
            at = (here + i) % PLANE
            push(
                xsend.at[c, pl.ds(pl.multiple_of(at * SUB, SUB), SUB), :], landing,
                rp_send, rp_recv.at[c], device(at % NX, at // NX, z, core),
            )

        if c >= LAG:
            finish(c - LAG)
    for c in range(CHUNKS - LAG, CHUNKS):
        finish(c)

    take(plane_in.at[pl.ds(0, PLANE - 1)], p_send)
    take(recv.at[:, pl.ds(0, NZ - 1)], z_send)
    take(z_back.at[:, pl.ds(0, rows - per_z), :], rz_send)
    take(back.at[:, pl.ds(0, (PLANE - 1) * SUB), :], rp_send)
    take(gate_up.at[pl.ds(0, 2)], g_send)
    take(down.at[pl.ds(0, 2)], d_send)
    for d in ORDER:
        s = (x + d) % NX
        for p in range(len(PIECES)):
            take(landed(s, p, core), gf_send.at[s, p])
        for c in range(CHUNKS):
            take(down_half(s, c, core), df_send.at[s, c])


def local(tokens, router_weight, gate_weight, up_weight, down_weight, routing, lengths):
    tok_dev, width = tokens.shape
    top_count = routing.shape[1]
    experts = gate_weight.shape[0] * lax.axis_size("seq")
    depth = gate_weight.shape[1]
    cap = max(2, tok_dev * top_count // experts + 1)
    rows = PLANE * NZ * cap
    wide = width // CHUNKS
    vmem = pl.BlockSpec(memory_space=pltpu.VMEM)
    hbm = pl.BlockSpec(memory_space=pltpu.HBM)
    sem = pltpu.SemaphoreType.DMA
    bf16 = jnp.bfloat16
    return pl.pallas_call(
        kernel,
        out_shape=jax.ShapeDtypeStruct((tok_dev, width), bf16),
        in_specs=[hbm] * 7,
        out_specs=vmem,
        scratch_shapes=[
            pltpu.SMEM(lengths.shape, jnp.int32),
            pltpu.VMEM((tok_dev, width), bf16),
            pltpu.VMEM((experts, width), bf16),
            pltpu.VMEM((top_count, tok_dev), jnp.int32),
            pltpu.VMEM((tok_dev, width), bf16),
            pltpu.VMEM((tok_dev, PLANE * SUB), bf16),
            pltpu.VMEM((tok_dev, PLANE * SUB), bf16),
            pltpu.VMEM((rows, rows), bf16),
            pltpu.VMEM((PLANE * SUB, rows), bf16),
            pltpu.VMEM((PLANE, NLO, cap, SUB, LANE), bf16),
            pltpu.VMEM((PLANE, NLO, cap, SUB, LANE), bf16),
            pltpu.VMEM((NY, NZ, NX, cap, SUB, LANE), bf16),
            pltpu.VMEM((rows, width), bf16),
            pltpu.VMEM((NX, 2, depth, width), bf16),
            pltpu.VMEM((NX, depth, width), bf16),
            pltpu.VMEM((NX, rows, depth), jnp.float32),
            pltpu.VMEM((NX, rows, depth), bf16),
            pltpu.VMEM((NX, rows, depth), bf16),
            pltpu.VMEM((PLANE * NLO * cap * SUB, LANE), jnp.float32),
            pltpu.VMEM((CHUNKS, rows, wide), bf16),
            pltpu.VMEM((CHUNKS, rows, wide), bf16),
            pltpu.VMEM((CHUNKS, PLANE * SUB, wide), bf16),
            pltpu.VMEM((CHUNKS, PLANE * SUB, wide), bf16),
            sem, *[sem((NX, len(PIECES)))] * 3,
            sem, sem((NX, CHUNKS)), sem((NX, CHUNKS)), sem((NX, CHUNKS)),
            sem, sem((NY,)), sem, sem((NY,)),
            sem, sem((CHUNKS,)), sem, sem((CHUNKS,)), sem((4,)),
        ],
        compiler_params=pltpu.CompilerParams(
            collective_id=0, has_side_effects=True, vmem_limit_bytes=60 * 1024 * 1024
        ),
    )(lengths, tokens, router_weight.T, routing.T, gate_weight, up_weight, down_weight)


def solution(mesh):
    in_specs = (
        P(("teacher", "seq"), None),
        P(),
        P("seq", "teacher", None),
        P("seq", "teacher", None),
        P("seq", "teacher", None),
        P(("teacher", "seq"), None),
        P(),
    )
    out_specs = P(("teacher", "seq"), None)
    return jax.shard_map(local, mesh=mesh, in_specs=in_specs, out_specs=out_specs, check_vma=False)
```

```python
import jax
import jax.numpy as jnp
from jax import lax
from jax.experimental import pallas as pl
from jax.experimental.pallas import tpu as pltpu
from jax.sharding import PartitionSpec as P

MESH = pl.DeviceIdType.MESH
NX, NY, NZ, NLO = 4, 4, 8, 4
PLANE = NX * NY
LANE = 128
SUB = 16
CHUNKS = 8
ORDER = (1, 3, 2)
LAG = 2
BEFORE = 2
PIECES = ((0, 0, 2), (1, 0, 1), (1, 1, 1))


def device(x, y, z, core):
    return ((z // NLO) * NX + x, (y * NLO + z % NLO) * 2 + core)


def split(values, by):
    if by == 16:
        whole = lax.shift_right_logical(values, 4)
    else:
        whole = lax.shift_right_logical(values * 171, {3: 9, 12: 11, 48: 13}[by])
    return whole, values - whole * by


def slot_columns(shape, per_place, cap):
    place, left = split(lax.broadcasted_iota(jnp.int32, shape, 1), per_place)
    z_lo, rank = split(left, cap)
    y, x = lax.shift_right_logical(place, 2), place & (NX - 1)
    expert = jnp.where(left < NLO * cap, (y * NLO + z_lo) * NX + x, -1)
    return expert, rank


def copy(src, dst, sem):
    return pltpu.make_async_copy(src, dst, sem)


def push(src, dst, send_sem, recv_sem, to):
    pltpu.make_async_remote_copy(
        src_ref=src, dst_ref=dst, send_sem=send_sem, recv_sem=recv_sem,
        device_id=to, device_id_type=MESH,
    ).start()


def take(ref, sem):
    pltpu.make_async_copy(ref, ref, sem).wait()


def kernel(
    lengths_hbm, tok_hbm, router_hbm, routing_hbm, gate_ref, up_ref, down_ref, out_ref,
    lengths_ref, tok_ref, router_ref, routing_ref, normed, mix_hi, mix_lo, order, gather, send1, plane_in, recv, rows_in, gate_up, down,
    gates, hidden, sorted_hidden, stage, rsend, z_back, xsend, back,
    g_send, g_recv, gf_send, gf_recv, d_send, d_recv, df_send, df_recv,
    p_send, p_recv, z_send, z_recv, rz_send, rz_recv, rp_send, rp_recv, in_sem,
):
    f32, bf16 = jnp.float32, jnp.bfloat16
    teacher, seq = lax.axis_index("teacher"), lax.axis_index("seq")
    x, z_hi = teacher % NX, teacher // NX
    core, z_lo, y = seq % 2, (seq // 2) % NLO, seq // (2 * NLO)
    z = z_hi * NLO + z_lo
    here = y * NX + x
    sibling = device(x, y, z, 1 - core)
    tokens, width = tok_ref.shape
    depth = gate_ref.shape[1]
    half = depth // 2
    cap = send1.shape[2]
    wide = width // CHUNKS
    rows = rows_in.shape[0]
    group = rows // NY
    per_z = rows // NZ

    own = (
        (tok_hbm, tok_ref), (lengths_hbm, lengths_ref), (routing_hbm, routing_ref),
        (router_hbm, router_ref),
    )
    for n, (src, dst) in enumerate(own):
        copy(src, dst, in_sem.at[n]).start()

    barrier = pltpu.get_barrier_semaphore()

    def greet(to):
        pl.semaphore_signal(barrier, inc=1, device_id=to, device_id_type=MESH)

    @pl.loop(1, NZ)
    def _(i):
        greet(device(x, y, (z + i) % NZ, core))

    @pl.loop(1, PLANE)
    def _(i):
        at = (here + i) % PLANE
        greet(device(at % NX, at // NX, z, core))

    @pl.loop(0, NX)
    def _(px):
        greet(device(px, y, z, 1 - core))

    def piece(p, part):
        m, start, count = PIECES[p]
        return m, pl.ds(part * half + start * (half // 2), count * (half // 2))

    def send_gate_up(i, p, part):
        m, at = piece(p, part)
        src = (gate_ref, up_ref)[m].at[i, at, :]
        dst = gate_up.at[x, m, at, :]
        goal = 2 * core + i

        @pl.when(goal != x)
        def _():
            push(src, dst, g_send, g_recv.at[x, p], device(goal, y, z, part))

        @pl.when(goal == x)
        def _():
            copy(src, dst, g_recv.at[x, p]).start()
            push(src, dst, g_send, g_recv.at[x, p], sibling)

    def send_down(i, c, part):
        goal = 2 * core + i
        at, cols = pl.ds(part * half, half), pl.ds(c * wide, wide)

        @pl.when(goal != x)
        def _():
            push(
                down_ref.at[i, at, cols], down.at[x, at, cols], d_send, d_recv.at[x, c],
                device(goal, y, z, part),
            )

        @pl.when(goal == x)
        def _():
            copy(down_ref.at[i, at, cols], down.at[x, at, cols], d_recv.at[x, c]).start()
            push(down_ref.at[i, at, cols], down.at[x, at, cols], d_send, d_recv.at[x, c], sibling)

    for n in range(3):
        copy(*own[n], in_sem.at[n]).wait()
    values = tok_ref[...].astype(f32)
    scale = lax.rsqrt(jnp.mean(values * values, axis=-1, keepdims=True) + 1e-06)
    normed[...] = (values * scale).astype(bf16)

    pl.semaphore_wait(barrier, NX + PLANE - 1 + NZ - 1)
    block = teacher * (2 * NLO * NY) + seq
    first = (block % 4) * tokens
    limit = lengths_ref[block // 4]
    live = first + lax.broadcasted_iota(jnp.int32, (tokens, 1), 0) < limit
    square = (tokens, tokens)
    diagonal = lax.broadcasted_iota(jnp.int32, square, 0) == lax.broadcasted_iota(
        jnp.int32, square, 1
    )

    def upright(row):
        return jnp.sum(jnp.where(diagonal, row, 0), axis=1, keepdims=True)

    name0, name1 = upright(routing_ref[0:1, :]), upright(routing_ref[1:2, :])
    earlier = (
        lax.broadcasted_iota(jnp.int32, square, 0) > lax.broadcasted_iota(jnp.int32, square, 1)
    ).astype(f32).astype(bf16)

    def slots(count, per_place):
        expert, rank = slot_columns((tokens, count), per_place, cap)
        named = jnp.logical_or(name0 == expert, name1 == expert)
        hit = jnp.where(jnp.logical_and(named, live), 1.0, 0.0)
        before = jnp.dot(earlier, hit.astype(bf16), preferred_element_type=f32)
        return expert, jnp.where(before == rank.astype(f32), hit, 0.0)

    _, chosen = slots(PLANE * NLO * cap, NLO * cap)
    picked = lax.dot_general(
        chosen.astype(bf16), normed[...], (((0,), (0,)), ((), ())), preferred_element_type=f32
    )
    for k in range(SUB):
        stage[pl.ds(k, PLANE * NLO * cap, stride=SUB), :] = picked[:, k * LANE:(k + 1) * LANE]
    send1[...] = stage[...].astype(bf16).reshape(send1.shape)

    copy(send1.at[here], plane_in.at[here], p_recv.at[y]).start()

    @pl.loop(1, PLANE)
    def _(i):
        px, py = (x + i) % NX, (y + i // NX) % NY
        push(
            send1.at[py * NX + px], plane_in.at[here], p_send, p_recv.at[y],
            device(px, py, z, core),
        )

    for p in range(len(PIECES)):
        for part in range(2):
            for i in range(2):
                send_gate_up(i, p, part)
    @pl.loop(0, NY)
    def _(i):
        g = (y + NY - i) % NY
        at = pl.ds(g * NX, NX)
        take(plane_in.at[at], p_recv.at[g])
        copy(plane_in.at[at, z_lo], recv.at[g, z], z_recv.at[g]).start()

        @pl.loop(1, NZ)
        def _(j):
            pz = (z + NZ // 2 + (1 - 2 * (j % 2)) * (j // 2)) % NZ
            push(
                plane_in.at[at, pz % NLO], recv.at[g, z], z_send, z_recv.at[g],
                device(x, y, pz, core),
            )

    for c in range(CHUNKS):
        for part in range(2):
            for i in range(2):
                send_down(i, c, part)

    copy(*own[3], in_sem.at[3]).wait()
    logits = lax.dot_general(
        normed[...], router_ref[...], (((1,), (1,)), ((), ())), preferred_element_type=f32
    )
    ids = lax.broadcasted_iota(jnp.int32, logits.shape, 1)

    def score(name):
        return jax.nn.sigmoid(
            jnp.sum(jnp.where(name == ids, logits, 0.0), axis=1, keepdims=True)
        )

    score0, score1 = score(name0), score(name1)
    both = score0 + score1
    expert, used = slots(PLANE * SUB, SUB)
    mix = used * jnp.where(name0 == expert, score0 / both, score1 / both)
    high = mix.astype(bf16)
    mix_hi[...] = high
    mix_lo[...] = (mix - high.astype(f32)).astype(bf16)

    i_at, q = split(lax.broadcasted_iota(jnp.int32, (rows, rows), 0), per_z)
    by_y, rest = split(q, NX * cap)
    column = lax.broadcasted_iota(jnp.int32, (rows, rows), 1)
    turn = (y + NY - by_y) & (NY - 1)
    order[...] = (turn * group + i_at * (NX * cap) + rest == column).astype(f32).astype(bf16)
    place, left = split(lax.broadcasted_iota(jnp.int32, (PLANE * SUB, rows), 0), SUB)
    from_z, q = split(lax.broadcasted_iota(jnp.int32, (PLANE * SUB, rows), 1), per_z)
    to_place, rank = split(q, cap)
    same = jnp.logical_and(place == to_place, left == (from_z & (NLO - 1)) * cap + rank)
    gather[...] = same.astype(f32).astype(bf16)

    def relayout(i):
        g = (y + NY - i) % NY
        take(recv.at[g], z_recv.at[g])
        part = pl.ds(0, group * SUB)
        stage[part, :] = recv[g].reshape(group * SUB, LANE).astype(f32)
        at = slice(i * group, (i + 1) * group)
        for k in range(SUB):
            rows_in[at, k * LANE:(k + 1) * LANE] = stage[
                pl.ds(k, group, stride=SUB), :
            ].astype(bf16)

    def times(s, m, at):
        return lax.dot_general(
            rows_in[at, :], gate_up[s, m], (((1,), (1,)), ((), ())), preferred_element_type=f32
        )

    def first_gate(s, at):
        gates[s, at, :] = times(s, 0, at)

    def first_up(s, at):
        gate = gates[s, at, :]
        hidden[s, at, :] = (gate / (1.0 + jnp.exp(-gate)) * times(s, 1, at)).astype(bf16)

    def sort(s):
        sorted_hidden[s] = jnp.dot(
            order[...], hidden[s], preferred_element_type=f32
        ).astype(bf16)

    def down_half(s, c, part):
        return down.at[s, pl.ds(part * half, half), pl.ds(c * wide, wide)]

    def landed(s, p, part):
        m, at = piece(p, part)
        return gate_up.at[s, m, at, :]

    def forward(p):
        for d in ORDER:
            s = (x + d) % NX
            mine = landed(s, p, core)
            take(mine, g_recv.at[s, p])
            push(mine, mine, gf_send.at[s, p], gf_recv.at[s, p], sibling)

    def forwarded(p):
        for d in ORDER:
            s = (x + d) % NX
            take(landed(s, p, 1 - core), gf_recv.at[s, p])

    early, late, every = slice(0, 2 * group), slice(2 * group, 4 * group), slice(0, rows)
    for p, (m, _, count) in enumerate(PIECES):
        take(gate_up.at[x, m, pl.ds(0, count * half), :], g_recv.at[x, p])
    relayout(0)
    relayout(1)
    first_gate(x, early)
    first_up(x, early)
    forward(0)
    forwarded(0)

    @pl.loop(1, NX)
    def _(d):
        first_gate((x + d) % NX, early)

    forward(1)
    relayout(2)
    relayout(3)
    first_gate(x, late)
    first_up(x, late)
    sort(x)

    forward(2)

    @pl.loop(1, NX)
    def _(d):
        first_gate((x + d) % NX, late)

    forwarded(1)
    forwarded(2)

    def last_up(d):
        s = (x + d) % NX
        first_up(s, every)
        sort(s)

    def forward_down(c):
        for d in ORDER:
            s = (x + d) % NX
            mine = down_half(s, c, core)
            take(mine, d_recv.at[s, c])
            push(mine, mine, df_send.at[s, c], df_recv.at[s, c], sibling)

    pl.loop(1, BEFORE)(last_up)
    forward_down(0)
    pl.loop(BEFORE, NX)(last_up)

    for c in range(CHUNKS):
        if c > 0:
            forward_down(c)
        cols = pl.ds(c * wide, wide)
        take(down.at[x, :, cols], d_recv.at[x, c])
        for d in ORDER:
            s = (x + d) % NX
            take(down_half(s, c, 1 - core), df_recv.at[s, c])

        @pl.loop(0, rows // 128)
        def _(b):
            at = pl.ds(pl.multiple_of(b * 128, 128), 128)
            total = jnp.zeros((128, wide), f32)
            for s in range(NX):
                total += jnp.dot(
                    sorted_hidden[s, at, :], down[s, :, c * wide:(c + 1) * wide],
                    preferred_element_type=f32,
                )
            rsend[c, at, :] = total.astype(bf16)

        def mine_of(pz):
            return rsend.at[c, pl.ds(pl.multiple_of(pz * per_z, per_z), per_z), :]

        copy(mine_of(z), z_back.at[c, pl.ds(pl.multiple_of(z * per_z, per_z), per_z), :],
             rz_recv.at[c]).start()

        @pl.loop(1, NZ)
        def _(j):
            pz = (z + NZ // 2 + (1 - 2 * (j % 2)) * (j // 2)) % NZ
            push(
                mine_of(pz),
                z_back.at[c, pl.ds(pl.multiple_of(z * per_z, per_z), per_z), :],
                rz_send, rz_recv.at[c], device(x, y, pz, core),
            )

    def finish(c):
        take(back.at[c], rp_recv.at[c])
        total = jnp.dot(mix_hi[...], back[c], preferred_element_type=f32)
        total += jnp.dot(mix_lo[...], back[c], preferred_element_type=f32)
        out_ref[:, c * wide:(c + 1) * wide] = total.astype(bf16)

    for c in range(CHUNKS):
        take(z_back.at[c], rz_recv.at[c])
        xsend[c] = jnp.dot(gather[...], z_back[c], preferred_element_type=f32).astype(bf16)
        landing = back.at[c, pl.ds(pl.multiple_of(here * SUB, SUB), SUB), :]
        copy(
            xsend.at[c, pl.ds(pl.multiple_of(here * SUB, SUB), SUB), :], landing, rp_recv.at[c]
        ).start()

        @pl.loop(1, PLANE)
        def _(i):
            at = (here + i) % PLANE
            push(
                xsend.at[c, pl.ds(pl.multiple_of(at * SUB, SUB), SUB), :], landing,
                rp_send, rp_recv.at[c], device(at % NX, at // NX, z, core),
            )

        if c >= LAG:
            finish(c - LAG)
    for c in range(CHUNKS - LAG, CHUNKS):
        finish(c)

    take(plane_in.at[pl.ds(0, PLANE - 1)], p_send)
    take(recv.at[:, pl.ds(0, NZ - 1)], z_send)
    take(z_back.at[:, pl.ds(0, rows - per_z), :], rz_send)
    take(back.at[:, pl.ds(0, (PLANE - 1) * SUB), :], rp_send)
    take(gate_up.at[pl.ds(0, 2)], g_send)
    take(down.at[pl.ds(0, 2)], d_send)
    for d in ORDER:
        s = (x + d) % NX
        for p in range(len(PIECES)):
            take(landed(s, p, core), gf_send.at[s, p])
        for c in range(CHUNKS):
            take(down_half(s, c, core), df_send.at[s, c])


def local(tokens, router_weight, gate_weight, up_weight, down_weight, routing, lengths):
    tok_dev, width = tokens.shape
    top_count = routing.shape[1]
    experts = gate_weight.shape[0] * lax.axis_size("seq")
    depth = gate_weight.shape[1]
    cap = max(2, tok_dev * top_count // experts + 1)
    rows = PLANE * NZ * cap
    wide = width // CHUNKS
    vmem = pl.BlockSpec(memory_space=pltpu.VMEM)
    hbm = pl.BlockSpec(memory_space=pltpu.HBM)
    sem = pltpu.SemaphoreType.DMA
    bf16 = jnp.bfloat16
    return pl.pallas_call(
        kernel,
        out_shape=jax.ShapeDtypeStruct((tok_dev, width), bf16),
        in_specs=[hbm] * 7,
        out_specs=vmem,
        scratch_shapes=[
            pltpu.SMEM(lengths.shape, jnp.int32),
            pltpu.VMEM((tok_dev, width), bf16),
            pltpu.VMEM((experts, width), bf16),
            pltpu.VMEM((top_count, tok_dev), jnp.int32),
            pltpu.VMEM((tok_dev, width), bf16),
            pltpu.VMEM((tok_dev, PLANE * SUB), bf16),
            pltpu.VMEM((tok_dev, PLANE * SUB), bf16),
            pltpu.VMEM((rows, rows), bf16),
            pltpu.VMEM((PLANE * SUB, rows), bf16),
            pltpu.VMEM((PLANE, NLO, cap, SUB, LANE), bf16),
            pltpu.VMEM((PLANE, NLO, cap, SUB, LANE), bf16),
            pltpu.VMEM((NY, NZ, NX, cap, SUB, LANE), bf16),
            pltpu.VMEM((rows, width), bf16),
            pltpu.VMEM((NX, 2, depth, width), bf16),
            pltpu.VMEM((NX, depth, width), bf16),
            pltpu.VMEM((NX, rows, depth), jnp.float32),
            pltpu.VMEM((NX, rows, depth), bf16),
            pltpu.VMEM((NX, rows, depth), bf16),
            pltpu.VMEM((PLANE * NLO * cap * SUB, LANE), jnp.float32),
            pltpu.VMEM((CHUNKS, rows, wide), bf16),
            pltpu.VMEM((CHUNKS, rows, wide), bf16),
            pltpu.VMEM((CHUNKS, PLANE * SUB, wide), bf16),
            pltpu.VMEM((CHUNKS, PLANE * SUB, wide), bf16),
            sem, *[sem((NX, len(PIECES)))] * 3,
            sem, sem((NX, CHUNKS)), sem((NX, CHUNKS)), sem((NX, CHUNKS)),
            sem, sem((NY,)), sem, sem((NY,)),
            sem, sem((CHUNKS,)), sem, sem((CHUNKS,)), sem((4,)),
        ],
        compiler_params=pltpu.CompilerParams(
            collective_id=0, has_side_effects=True, vmem_limit_bytes=60 * 1024 * 1024
        ),
    )(lengths, tokens, router_weight.T, routing.T, gate_weight, up_weight, down_weight)


def solution(mesh):
    in_specs = (
        P(("teacher", "seq"), None),
        P(),
        P("seq", "teacher", None),
        P("seq", "teacher", None),
        P("seq", "teacher", None),
        P(("teacher", "seq"), None),
        P(),
    )
    out_specs = P(("teacher", "seq"), None)
    return jax.shard_map(local, mesh=mesh, in_specs=in_specs, out_specs=out_specs, check_vma=False)
```
